32 devices in a mesh: lat: 8 (over z, x), rad: 4 (over y, core).
Axes of the slice: x: 2, y: 2, z: 4, core: 2. Of those that a mesh axis runs over, the one named last changes fastest.
Arguments:
- kernel: bfloat16 [1024, 4, 64, 256], P(('lat', 'rad')), may hold values from -0.1875 to 0.1875
- target_device: int32 [1024, 4], P(('lat', 'rad')), may hold values from 0 to 31, all different within a row; in each aligned block of 32 rows (0 to 31, 32 to 63, ...) at most 8 rows name the same one
- target_block: int32 [1024, 4], P(('lat', 'rad')), may hold values from 0 to 127
- counts: int32 [1024], P(('lat', 'rad')), may hold values from 16 to 64
- traveltimes: float32 [1024, 64], P(('lat', 'rad')), may hold values from -6 to 6
- prior_residual: float32 [1024, 64], P(('lat', 'rad')), may hold values from -12 to 12
Outputs:
- model_update: float32 [32, 128, 256], P('rad', 'lat')
- data_vector: float32 [1024, 64], P(('lat', 'rad'))
The draws below stay inside these ranges and needn't reach their ends.
Inputs may be any that keep to these rules, and one draw needn't show every extreme that they name: `target_device`: each ray block names 4 different devices; among the ray blocks of one device at most 8 name the same device, and some device is named by exactly 8 of them.
All inputs are finite; a program needn't handle non-finite values.
Results may differ from the reference program's by a relative error of at most 0.007.
Values may be sent and summed in bfloat16 or wider, within the bound.
A program may use at most 128 MiB of HBM per device.

```python
import math
import jax
import jax.numpy as jnp
import numpy as np
from jax import lax

RAYS = 64
CELLS = 256
K = 4
ITERS = 3
RB_DEV = 32
MB_R = 8
MB_L = 16
CAP = 8
NRB = 1024
N_LAT = 8
N_RAD = 4
DEVICES = 32


def place_ends(drawn, own_key, least, high):
    index_at = [jax.random.randint(jax.random.fold_in(own_key, axis), (), 0, length) for axis, length in enumerate(drawn.shape)]
    main_axis = drawn.shape.index(max(drawn.shape))
    beside = index_at[:main_axis] + [(index_at[main_axis] + 1) % drawn.shape[main_axis]] + index_at[main_axis + 1:]
    return drawn.at[tuple(index_at)].set(least).at[tuple(beside)].set(high)


def block_scale(rng, shape, split, low, high):
    level, own = 1.0, jax.random.fold_in(rng, 6)
    for dim, blocks in split:
        heights = jnp.exp(jax.random.uniform(jax.random.fold_in(own, dim), (blocks,), jnp.float32, low / len(split), high / len(split)))
        level = level * jnp.repeat(heights, shape[dim] // blocks).reshape([-1 if axis == dim else 1 for axis in range(len(shape))])
    return level


def routed_block(key, own, number, rows, count, top, bound, skew):
    sequence = jax.random.permutation(key, count)
    crowded, usual = shares(count, rows * top, bound, skew, True), shares(count, rows * top, bound, skew, False)
    places = jnp.arange(count)

    def named(lengths, turn):
        used = int((lengths > 0).sum())
        fixed = max(1, used // 4)
        passed = fixed + (places - fixed + turn * (used - fixed)) % max(1, count - fixed)
        return jnp.zeros((count,), jnp.int32).at[sequence[jnp.where(places < fixed, places, passed)]].set(jnp.asarray(lengths, jnp.int32))

    lengths = jnp.where(number % 4 == 0, named(crowded, number // 4), named(usual, number - number // 4 - 1))
    mixed = jax.random.permutation(jax.random.fold_in(own, 3), count)
    source_of, taker = mixed[0:count // 2 * 2:2], mixed[1:count // 2 * 2:2]
    slack = jnp.minimum(lengths[source_of] - 1, bound - lengths[taker]) // 2
    slack = jnp.where((source_of == sequence[0]) | (taker == sequence[0]) | (lengths[taker] == 0), 0, jnp.maximum(slack, 0))
    passed = jax.random.randint(jax.random.fold_in(own, 4), (count // 2,), 0, 1 << 20) % (slack + 1)
    lengths = lengths.at[source_of].add(-passed).at[taker].add(passed)
    labels = jnp.searchsorted(jnp.cumsum(lengths), jnp.arange(rows * top), side="right").astype(jnp.int32)
    table = labels.reshape(top, rows).T
    table = table[jax.random.permutation(jax.random.fold_in(own, 1), rows)]
    turn = jax.random.randint(jax.random.fold_in(own, 2), (rows, 1), 0, top)
    return jnp.take_along_axis(table, (jnp.arange(top)[None, :] + turn) % top, axis=1)


def shares(number_of, total, most, skew, full):
    loads = [(1 << 20) // math.isqrt(standing ** skew) + 1 for standing in range(1, number_of + 1)]
    largest = most if full else min(most, max(-(-total // number_of), total * loads[0] // sum(loads)))
    least = 1 if total - largest >= number_of - 1 else 0
    given, spare = [largest] + [least] * (number_of - 1), total - largest - least * (number_of - 1)
    while spare > 0:
        free = [i for i in range(1, number_of) if given[i] < largest] or [i for i in range(1, number_of) if given[i] < most]
        mass, left = sum([loads[i] for i in free]), spare
        for i in free:
            addition = min(most - given[i], max(1, left * loads[i] // mass), spare)
            given[i] = given[i] + addition
            spare = spare - addition
    return np.array(given)


def normal_values(rng, extent, spread, reach, shards=(), kind=jnp.bfloat16):
    entries = jax.random.normal(rng, extent, jnp.float32) * spread
    if len(shards) > 0:
        entries = block_scale(rng, extent, shards, -0.22, 0.18) * entries
    return jnp.clip(entries, min=-reach, max=reach).astype(kind)


def setup_inputs(seed: int = 0) -> dict:
    key_of = jax.random.split(jax.random.key(seed), 7)
    kernel = normal_values(key_of[0], (NRB, K, RAYS, CELLS), (K * CELLS) ** -0.5, 0.1875, ((0, 32),))
    target_device_keys = jax.random.split(jax.random.fold_in(key_of[1], 1), NRB // RB_DEV)
    target_device_turns = jax.random.permutation(jax.random.fold_in(key_of[1], 3), NRB // RB_DEV)
    target_device = jax.vmap(lambda own, number: routed_block(jax.random.fold_in(key_of[1], 2), own, number, RB_DEV, DEVICES, K, CAP, 2))(target_device_keys, target_device_turns).reshape((NRB, K))
    target_block = place_ends(jax.random.randint(key_of[2], (NRB, K), 0, MB_R * MB_L), jax.random.fold_in(key_of[2], 1), 0, (MB_R * MB_L) - 1).astype(jnp.int32)
    counts = place_ends(jax.random.randint(key_of[3], (NRB,), RAYS // 4, RAYS + 1), jax.random.fold_in(key_of[3], 1), RAYS // 4, RAYS).astype(jnp.int32)
    traveltimes = normal_values(key_of[4], (NRB, RAYS), 1.0, 6.0, ((0, 32),), jnp.float32)
    prior_residual = normal_values(key_of[5], (NRB, RAYS), 2.0, 12.0, ((0, 32),), jnp.float32)
    return dict(kernel=kernel, target_device=target_device, target_block=target_block, counts=counts, traveltimes=traveltimes, prior_residual=prior_residual)


FREEDOM = 4.0
DAMPING = 0.3

def block_index(target_device, target_block):
    lat_pos = target_device // N_RAD
    rad_pos = target_device % N_RAD
    row_index = rad_pos * MB_R + target_block // MB_L
    col_index = lat_pos * MB_L + target_block % MB_L
    return (row_index * (MB_L * N_LAT) + col_index).astype(jnp.int32)

def forward(kernel, index, model_field):
    flat_model = model_field.reshape(-1, CELLS).astype(jnp.bfloat16)
    groups = kernel.reshape(N_LAT * N_RAD, RB_DEV, K, RAYS, CELLS)
    lists = index.reshape(N_LAT * N_RAD, RB_DEV, K)

    def per_group(inputs_pair):
        tile_group, id_group = inputs_pair
        blocks = flat_model[id_group]
        return jnp.einsum('bkrc,bkc->br', tile_group.astype(jnp.float32), blocks.astype(jnp.float32))
    return lax.map(per_group, (groups, lists)).reshape(N_LAT * N_RAD * RB_DEV, RAYS)

def adjoint(kernel, index, ray_values):
    rounded = ray_values.astype(jnp.bfloat16).reshape(N_LAT * N_RAD, RB_DEV, RAYS)
    groups = kernel.reshape(N_LAT * N_RAD, RB_DEV, K, RAYS, CELLS)

    def per_group(inputs_pair):
        tile_group, row_group = inputs_pair
        return jnp.einsum('bkrc,br->bkc', tile_group.astype(jnp.float32), row_group.astype(jnp.float32))
    partial_value = lax.map(per_group, (groups, rounded))
    summed = jax.ops.segment_sum(partial_value.reshape(-1, CELLS), index.reshape(-1), num_segments=MB_R * N_RAD * MB_L * N_LAT)
    return summed.reshape(MB_R * N_RAD, MB_L * N_LAT, CELLS)

def roughen(model_field):
    padded = jnp.pad(model_field, ((1, 1), (1, 1), (0, 0)))
    beside = padded[2:, 1:-1] + padded[:-2, 1:-1] + padded[1:-1, 2:] + padded[1:-1, :-2]
    return 4.0 * model_field - beside

def reference(kernel, target_device, target_block, counts, traveltimes, prior_residual):
    index = block_index(target_device, target_block)
    ray_mask = (jnp.arange(RAYS, dtype=jnp.int32)[None, :] < counts[:, None]).astype(jnp.float32)
    weights = ray_mask * jnp.sqrt((FREEDOM + 1.0) / (FREEDOM + prior_residual * prior_residual))
    data_vector = weights * traveltimes
    beta_norm = jnp.sqrt(jnp.sum(data_vector * data_vector))
    data_vector = data_vector / beta_norm
    model_dir = adjoint(kernel, index, weights * data_vector)
    alpha_norm = jnp.sqrt(jnp.sum(model_dir * model_dir))
    model_dir = model_dir / alpha_norm
    pen_vec = jnp.zeros_like(model_dir)
    search_dir = model_dir
    model_update = jnp.zeros_like(model_dir)
    phi_bar = beta_norm
    rho_bar = alpha_norm
    for sweep in range(ITERS):
        data_vector = weights * forward(kernel, index, model_dir) - alpha_norm * data_vector
        pen_vec = DAMPING * roughen(model_dir) - alpha_norm * pen_vec
        beta_norm = jnp.sqrt(jnp.sum(data_vector * data_vector) + jnp.sum(pen_vec * pen_vec))
        data_vector = data_vector / beta_norm
        pen_vec = pen_vec / beta_norm
        model_dir = adjoint(kernel, index, weights * data_vector) + DAMPING * roughen(pen_vec) - beta_norm * model_dir
        alpha_norm = jnp.sqrt(jnp.sum(model_dir * model_dir))
        model_dir = model_dir / alpha_norm
        rho_value = jnp.sqrt(rho_bar * rho_bar + beta_norm * beta_norm)
        cosine = rho_bar / rho_value
        sine = beta_norm / rho_value
        theta_value = sine * alpha_norm
        rho_bar = -cosine * alpha_norm
        phi_value = cosine * phi_bar
        phi_bar = sine * phi_bar
        model_update = model_update + phi_value / rho_value * search_dir
        search_dir = model_dir - theta_value / rho_value * search_dir
    return (model_update, data_vector)
```

```python
import functools

import jax
import jax.numpy as jnp
from jax import lax
from jax.experimental import pallas as pl
from jax.experimental.pallas import tpu as pltpu
from jax.sharding import PartitionSpec as P

ITERS = 3
MB_R = 8
MB_L = 16
FREEDOM = 4.0
DAMPING = 0.3
LANES = 128
GROUP = 8

F32 = jnp.float32
BF16 = jnp.bfloat16
MESH = pl.DeviceIdType.MESH


def iota(shape, dim):
    return lax.broadcasted_iota(jnp.int32, shape, dim)


def onehot(cond):
    return jnp.where(cond, 1.0, 0.0).astype(BF16)


def lsqr_kernel(
    n_lat, n_rad, slots,
    kernel_ref, target_ref, block_ref, counts_ref, times_ref, prior_ref,
    update_ref, data_ref,
    tiles, send, recv, sum_send, sum_recv, edge_send, edge_recv, ids_send, ids_recv,
    tile_sem, send_sem, recv_sem, sum_send_sem, sum_recv_sem, edge_send_sem, edge_recv_sem,
    ids_send_sem, ids_recv_sem,
):
    n = n_lat * n_rad
    rays_b, fanout, ray_len, cells = tiles.shape
    entries = rays_b * fanout
    halves = cells // LANES
    rows = halves * slots
    num_blocks = MB_R * MB_L
    groups = rays_b // GROUP
    width = GROUP * ray_len
    lat, rad = lax.axis_index("lat"), lax.axis_index("rad")
    me = lat * n_rad + rad

    def at(peer):
        return (peer // n_rad, peer % n_rad)

    def shifted(step):
        return at(lax.rem(me + step, n))

    barrier = pltpu.get_barrier_semaphore()

    def greet(step, carry):
        pl.semaphore_signal(barrier, inc=1, device_id=shifted(step), device_id_type=MESH)
        return carry

    lax.fori_loop(1, n, greet, 0)

    def tile_copy(g):
        part = pl.ds(g * GROUP, GROUP)
        return pltpu.make_async_copy(kernel_ref.at[part], tiles.at[part], tile_sem.at[g])

    for g in range(groups):
        tile_copy(g).start()

    named = jnp.concatenate([target_ref[:, k:k + 1] for k in range(fanout)], axis=0)
    wanted = jnp.concatenate([block_ref[:, k:k + 1] for k in range(fanout)], axis=0)
    away = named - me
    away = jnp.where(away < 0, away + n, away)
    square = (entries, entries)
    away_col = jnp.broadcast_to(away.astype(F32), square)
    away_row = away_col.T
    earlier = (away_col == away_row) & (iota(square, 1) < iota(square, 0))
    rank = jnp.sum(jnp.where(earlier, 1.0, 0.0), axis=1, keepdims=True)
    place_col = away.astype(F32) * rows + rank
    place_row = jnp.broadcast_to(place_col, square).T[0:1, :]
    place_cols = jnp.concatenate([place_col + h * slots for h in range(halves)], axis=0)
    place_rows = jnp.concatenate([place_row + h * slots for h in range(halves)], axis=1)
    pick = onehot(
        iota((halves * entries, n * rows), 1) == place_cols.astype(jnp.int32)
    )
    spread = onehot(
        iota((n * rows, halves * entries), 0) == place_rows.astype(jnp.int32)
    )
    partner = onehot(iota((n, entries), 0) == away_row[0:1, :].astype(jnp.int32))
    marks = jnp.where(
        iota((entries, LANES), 1) == rank.astype(jnp.int32), (wanted + 1).astype(F32), 0.0
    ).astype(BF16)
    ids = jnp.dot(partner, marks, preferred_element_type=F32)

    lane = iota((GROUP, width), 1)
    own = (lane // ray_len) == iota((GROUP, width), 0)
    ray = lane % ray_len
    eye = iota((rays_b, rays_b), 0) == iota((rays_b, rays_b), 1)
    count = jnp.sum(
        jnp.where(eye, jnp.broadcast_to(counts_ref[...], (rays_b, rays_b)).astype(F32), 0.0),
        axis=1, keepdims=True,
    ).astype(jnp.int32)

    def repeated(ref, g):
        part = ref[g * GROUP:(g + 1) * GROUP, :]
        return jnp.concatenate([part] * GROUP, axis=1)

    weights, data = [], []
    for g in range(groups):
        prior = repeated(prior_ref, g)
        valid = own & (ray < count[g * GROUP:(g + 1) * GROUP])
        w = jnp.where(valid, jnp.sqrt((FREEDOM + 1.0) / (FREEDOM + prior * prior)), 0.0)
        weights.append(w)
        data.append(w * repeated(times_ref, g))

    def total(parts):
        acc = parts[0] * parts[0]
        for p in parts[1:]:
            acc = acc + p * p
        return jnp.sum(jnp.sum(acc, axis=0, keepdims=True), axis=1, keepdims=True)

    pl.semaphore_wait(barrier, n - 1)

    def exchange(src, dst, size, s_sem, r_sem):
        def go(step, carry):
            back = n - step
            pltpu.make_async_remote_copy(
                src_ref=src.at[pl.ds(pl.multiple_of(step * size, size), size)],
                dst_ref=dst.at[pl.ds(pl.multiple_of(back * size, size), size)],
                send_sem=s_sem, recv_sem=r_sem,
                device_id=shifted(step), device_id_type=MESH,
            ).start()
            return carry
        lax.fori_loop(1, n, go, 0)

    def arrived(dst, size, sem):
        part = dst.at[pl.ds(size, (n - 1) * size)]
        pltpu.make_async_copy(part, part, sem).wait()

    def send_sum(i, value):
        row = jnp.broadcast_to(value, (1, LANES))
        sum_send[i] = row
        sum_recv[i, 0] = row
        src, dst = sum_send.at[i], sum_recv.at[i]

        def go(step, carry):
            pltpu.make_async_remote_copy(
                src_ref=src, dst_ref=dst.at[n - step],
                send_sem=sum_send_sem.at[i], recv_sem=sum_recv_sem.at[i],
                device_id=shifted(step), device_id_type=MESH,
            ).start()
            return carry
        lax.fori_loop(1, n, go, 0)

    def get_sum(i):
        arrived(sum_recv.at[i], 1, sum_recv_sem.at[i])
        return jnp.sum(sum_recv[i], axis=0)[:, 0:1]

    field4 = (halves, MB_R, MB_L, LANES)
    field = (halves * num_blocks, LANES)
    radial, lateral = halves * MB_L, halves * MB_R
    edge_parts = ((0, radial), (radial, radial), (2 * radial, lateral), (2 * radial + lateral, lateral))
    up = (lat, lax.rem(rad + n_rad - 1, n_rad))
    down = (lat, lax.rem(rad + 1, n_rad))
    left = (lax.rem(lat + n_lat - 1, n_lat), rad)
    right = (lax.rem(lat + 1, n_lat), rad)

    def send_edges(i, x):
        x4 = x.reshape(field4)
        edge_send[i, 0:radial] = x4[:, 0].reshape(radial, LANES)
        edge_send[i, radial:2 * radial] = x4[:, MB_R - 1].reshape(radial, LANES)
        edge_send[i, 2 * radial:2 * radial + lateral] = x4[:, :, 0].reshape(lateral, LANES)
        edge_send[i, 2 * radial + lateral:] = x4[:, :, MB_L - 1].reshape(lateral, LANES)
        for a, b, device in ((0, 1, up), (1, 0, down), (2, 3, left), (3, 2, right)):
            pltpu.make_async_remote_copy(
                src_ref=edge_send.at[i, pl.ds(*edge_parts[a])],
                dst_ref=edge_recv.at[i, pl.ds(*edge_parts[b])],
                send_sem=edge_send_sem.at[i], recv_sem=edge_recv_sem.at[i],
                device_id=device, device_id_type=MESH,
            ).start()

    def roughen(i, x):
        whole = edge_recv.at[i]
        pltpu.make_async_copy(whole, whole, edge_recv_sem.at[i]).wait()

        def edge(part, outside):
            start, size = edge_parts[part]
            return jnp.where(outside, 0.0, edge_recv[i, start:start + size])

        above = edge(0, rad == 0).reshape(halves, 1, MB_L, LANES)
        below = edge(1, rad == n_rad - 1).reshape(halves, 1, MB_L, LANES)
        before = edge(2, lat == 0)
        after = edge(3, lat == n_lat - 1)
        x4 = x.reshape(field4)
        radials = jnp.concatenate([above, x4[:, :-1]], axis=1) + jnp.concatenate(
            [x4[:, 1:], below], axis=1
        )

        def along(e):
            return jnp.broadcast_to(e[:, None, :], (lateral, MB_L, LANES)).reshape(field)

        block_l = iota(field, 0) % MB_L
        prev = jnp.where(block_l == 0, along(before), pltpu.roll(x, 1, 0))
        nxt = jnp.where(block_l == MB_L - 1, along(after), pltpu.roll(x, field[0] - 1, 0))
        return 4.0 * x - (radials.reshape(field) + prev + nxt)

    def tile_part(g, k):
        return tiles[g * GROUP:(g + 1) * GROUP, k].reshape(width, cells)

    def send_rows(i, values):
        send[i] = values.astype(BF16)
        recv[i, 0:rows] = send[i, 0:rows]
        exchange(send.at[i], recv.at[i], rows, send_sem.at[i], recv_sem.at[i])

    def adjoint(i, ray_values, first=False):
        parts = [[None] * groups for _ in range(fanout)]
        for g in range(groups):
            if first:
                tile_copy(g).wait()
            y = ray_values[g].astype(BF16)
            for k in range(fanout):
                parts[k][g] = jnp.dot(y, tile_part(g, k), preferred_element_type=F32)
        flat = [p for k in range(fanout) for p in parts[k]]
        stacked = jnp.concatenate(
            [p[:, h * LANES:(h + 1) * LANES] for h in range(halves) for p in flat], axis=0
        ).astype(BF16)
        send_rows(i, jnp.dot(spread, stacked, preferred_element_type=F32))

    def forward(i):
        arrived(recv.at[i], rows, recv_sem.at[i])
        blocks = jnp.dot(pick, recv[i], preferred_element_type=F32)
        out = []
        for g in range(groups):
            acc = None
            for k in range(fanout):
                at_row = k * rays_b + g * GROUP
                v = jnp.concatenate(
                    [
                        blocks[h * entries + at_row:h * entries + at_row + GROUP]
                        for h in range(halves)
                    ],
                    axis=1,
                ).astype(BF16)
                term = lax.dot_general(
                    v, tile_part(g, k), (((1,), (1,)), ((), ())), preferred_element_type=F32
                )
                acc = term if acc is None else acc + term
            out.append(acc)
        return out

    first_sum = total(data)
    id_rows = jnp.where(iota((n, LANES), 1) == slots, first_sum, ids)
    ids_send[...] = id_rows.reshape(n, 1, LANES)
    ids_recv[0] = ids_send[0]
    exchange(ids_send, ids_recv, 1, ids_send_sem, ids_recv_sem)

    adjoint(0, [w * d for w, d in zip(weights, data)], first=True)

    arrived(ids_recv, 1, ids_recv_sem)
    got = ids_recv[...].reshape(n, LANES)
    beta = jnp.sqrt(jnp.sum(got, axis=0, keepdims=True)[:, slots:slots + 1])
    slot_rows = (n * rows, LANES)
    each = jnp.broadcast_to(got[:, None, :], (n, rows, LANES)).reshape(slot_rows)
    each = jnp.where(iota(slot_rows, 1) == iota(slot_rows, 0) % slots, each, 0.0)
    block_id = jnp.sum(each, axis=1, keepdims=True).astype(jnp.int32)
    asked = jnp.where(iota(slot_rows, 1) + 1 == block_id, 1.0, 0.0)
    half = (iota(slot_rows, 0) % rows) // slots
    served = jnp.concatenate([jnp.where(half == h, asked, 0.0) for h in range(halves)], axis=1)
    gather = served.astype(BF16)
    collect = served.T.astype(BF16)

    def collected(i):
        arrived(recv.at[i], rows, recv_sem.at[i])
        return jnp.dot(collect, recv[i], preferred_element_type=F32)

    x = collected(0) / beta
    data = [d / beta for d in data]
    phi_bar = beta
    round_i, sum_i, edge_i = 1, 0, 0
    pen = search = update = None
    for sweep in range(ITERS):
        send_rows(round_i, jnp.dot(gather, x.astype(BF16), preferred_element_type=F32))
        send_edges(edge_i, x)
        send_sum(sum_i, total([x]))
        products = forward(round_i)
        alpha = jnp.sqrt(get_sum(sum_i))
        inverse = 1.0 / alpha
        data = [w * (p * inverse) - alpha * d for w, p, d in zip(weights, products, data)]
        v = x * inverse
        pen_new = (DAMPING * inverse) * roughen(edge_i, x)
        pen = pen_new if pen is None else pen_new - alpha * pen
        round_i, sum_i, edge_i = round_i + 1, sum_i + 1, edge_i + 1
        if sweep == 0:
            search = v
            rho_bar = alpha
        else:
            search = v - (sine * alpha / rho) * search
            rho_bar = -cosine * alpha
        last = sweep == ITERS - 1
        acc = total(data) + total([pen])
        send_sum(sum_i, acc)
        if not last:
            send_edges(edge_i, pen)
            adjoint(round_i, [w * d for w, d in zip(weights, data)])
        beta = jnp.sqrt(get_sum(sum_i))
        inverse = 1.0 / beta
        data = [d * inverse for d in data]
        rho = jnp.sqrt(rho_bar * rho_bar + beta * beta)
        cosine, sine = rho_bar / rho, beta / rho
        phi = cosine * phi_bar
        phi_bar = sine * phi_bar
        step = (phi / rho) * search
        update = step if update is None else update + step
        if not last:
            rough = DAMPING * roughen(edge_i, pen)
            pen = pen * inverse
            x = (collected(round_i) + rough) * inverse - beta * v
            round_i, edge_i = round_i + 1, edge_i + 1
        sum_i += 1

    for h in range(halves):
        part = update[h * num_blocks:(h + 1) * num_blocks]
        update_ref[:, :, h * LANES:(h + 1) * LANES] = part.reshape(MB_R, MB_L, LANES)
    for g in range(groups):
        acc = data[g][:, 0:ray_len]
        for i in range(1, GROUP):
            acc = acc + data[g][:, i * ray_len:(i + 1) * ray_len]
        data_ref[g * GROUP:(g + 1) * GROUP, :] = acc

    def left_buffer(ref, sem):
        pltpu.make_async_copy(ref, ref, sem).wait()

    left_buffer(ids_send.at[pl.ds(1, n - 1)], ids_send_sem)
    for i in range(2 * ITERS):
        left_buffer(send.at[i, pl.ds(rows, (n - 1) * rows)], send_sem.at[i])
    for i in range(2 * ITERS):
        left_buffer(sum_recv.at[i, pl.ds(1, n - 1)], sum_send_sem.at[i])
    for i in range(2 * ITERS - 1):
        left_buffer(edge_send.at[i], edge_send_sem.at[i])


def body(kernel, target_device, target_block, counts, traveltimes, prior_residual):
    n_lat, n_rad = lax.axis_size("lat"), lax.axis_size("rad")
    n = n_lat * n_rad
    rays_b, fanout, ray_len, cells = kernel.shape
    capacity = max(2, 2 * rays_b * fanout // n)
    slots = -(-capacity // 8) * 8
    halves = cells // LANES
    rows = halves * slots
    edges = 2 * halves * (MB_R + MB_L)
    payloads, sums, fields = 2 * ITERS, 2 * ITERS, 2 * ITERS - 1
    dma = pltpu.SemaphoreType.DMA
    vmem = pl.BlockSpec(memory_space=pltpu.VMEM)
    return pl.pallas_call(
        functools.partial(lsqr_kernel, n_lat, n_rad, slots),
        out_shape=(
            jax.ShapeDtypeStruct((MB_R, MB_L, cells), F32),
            jax.ShapeDtypeStruct((rays_b, ray_len), F32),
        ),
        in_specs=[pl.BlockSpec(memory_space=pl.ANY)] + [vmem] * 5,
        out_specs=(vmem, vmem),
        scratch_shapes=[
            pltpu.VMEM(kernel.shape, BF16),
            pltpu.VMEM((payloads, n * rows, LANES), BF16),
            pltpu.VMEM((payloads, n * rows, LANES), BF16),
            pltpu.VMEM((sums, 1, LANES), F32),
            pltpu.VMEM((sums, n, 1, LANES), F32),
            pltpu.VMEM((fields, edges, LANES), F32),
            pltpu.VMEM((fields, edges, LANES), F32),
            pltpu.VMEM((n, 1, LANES), F32),
            pltpu.VMEM((n, 1, LANES), F32),
            dma((rays_b // GROUP,)),
            dma((payloads,)), dma((payloads,)),
            dma((sums,)), dma((sums,)),
            dma((fields,)), dma((fields,)),
            dma, dma,
        ],
        compiler_params=pltpu.CompilerParams(
            collective_id=0, has_side_effects=True, vmem_limit_bytes=48 * 1024 * 1024
        ),
        cost_estimate=pl.CostEstimate(
            flops=14 * kernel.size, bytes_accessed=2 * kernel.size, transcendentals=0
        ),
    )(kernel, target_device, target_block, counts.reshape(1, rays_b), traveltimes, prior_residual)


def solution(mesh):
    in_specs = (
        P(("lat", "rad"), None, None, None),
        P(("lat", "rad"), None),
        P(("lat", "rad"), None),
        P(("lat", "rad")),
        P(("lat", "rad"), None),
        P(("lat", "rad"), None),
    )
    out_specs = (P("rad", "lat", None), P(("lat", "rad"), None))
    return jax.shard_map(body, mesh=mesh, in_specs=in_specs, out_specs=out_specs, check_vma=False)
```

```python
import functools

import jax
import jax.numpy as jnp
from jax import lax
from jax.experimental import pallas as pl
from jax.experimental.pallas import tpu as pltpu
from jax.sharding import PartitionSpec as P

ITERS = 3
MB_R = 8
MB_L = 16
FREEDOM = 4.0
DAMPING = 0.3
LANES = 128
GROUP = 8

F32 = jnp.float32
BF16 = jnp.bfloat16
MESH = pl.DeviceIdType.MESH


def iota(shape, dim):
    return lax.broadcasted_iota(jnp.int32, shape, dim)


def onehot(cond):
    return jnp.where(cond, 1.0, 0.0).astype(BF16)


def lsqr_kernel(
    n_lat, n_rad, slots,
    kernel_ref, target_hbm, block_hbm, counts_hbm, times_hbm, prior_hbm,
    update_ref, data_ref,
    tiles, target_ref, block_ref, counts_ref, times_ref, prior_ref,
    send, recv, rad_send, rad_recv, lat_send, lat_recv,
    edge_send, edge_recv, ids_send, ids_recv,
    tile_sem, small_sem, send_sem, recv_sem, rad_send_sem, rad_recv_sem,
    lat_send_sem, lat_recv_sem, edge_send_sem, edge_recv_sem, ids_send_sem, ids_recv_sem,
):
    n = n_lat * n_rad
    rays_b, fanout, ray_len, cells = tiles.shape
    entries = rays_b * fanout
    halves = cells // LANES
    rows = halves * slots
    num_blocks = MB_R * MB_L
    groups = rays_b // GROUP
    width = GROUP * ray_len
    lat, rad = lax.axis_index("lat"), lax.axis_index("rad")

    small = (
        (target_hbm, target_ref), (block_hbm, block_ref), (counts_hbm, counts_ref),
        (times_hbm, times_ref), (prior_hbm, prior_ref),
    )
    for i, (src, dst) in enumerate(small):
        pltpu.make_async_copy(src, dst, small_sem.at[i]).start()

    def tile_copy(g):
        part = pl.ds(g * GROUP, GROUP)
        return pltpu.make_async_copy(kernel_ref.at[part], tiles.at[part], tile_sem.at[g])

    for g in range(groups):
        tile_copy(g).start()

    rads = [lax.rem(rad + dr, n_rad) for dr in range(n_rad)]

    def each_lat(act):
        def go(dl, carry):
            act(dl, lax.rem(lat + dl, n_lat))
            return carry
        lax.fori_loop(1, n_lat, go, 0)

    def each_partner(act):
        for dr in range(1, n_rad):
            act(dr, n_rad - dr, (lat, rads[dr]))

        def row(dl, peer):
            here, there = dl * n_rad, (n_lat - dl) * n_rad
            for dr in range(n_rad):
                act(here + dr, there + (n_rad - dr) % n_rad, (peer, rads[dr]))
        each_lat(row)

    barrier = pltpu.get_barrier_semaphore()
    each_partner(
        lambda here, there, device: pl.semaphore_signal(
            barrier, inc=1, device_id=device, device_id_type=MESH
        )
    )
    for i, (src, dst) in enumerate(small):
        pltpu.make_async_copy(src, dst, small_sem.at[i]).wait()

    square = (entries, entries)
    named = jnp.concatenate([target_ref[k:k + 1, :] for k in range(fanout)], axis=1)
    wanted = jnp.concatenate([block_ref[k:k + 1, :] for k in range(fanout)], axis=1)
    away_lat = named // n_rad - lat
    away_rad = named % n_rad - rad
    away_lat = jnp.where(away_lat < 0, away_lat + n_lat, away_lat)
    away_rad = jnp.where(away_rad < 0, away_rad + n_rad, away_rad)
    away_row = jnp.broadcast_to((away_lat * n_rad + away_rad).astype(F32), square)
    away_col = away_row.T
    wanted = jnp.broadcast_to(wanted.astype(F32), square).T[:, 0:1]
    earlier = (away_col == away_row) & (iota(square, 1) < iota(square, 0))
    rank = jnp.sum(jnp.where(earlier, 1.0, 0.0), axis=1, keepdims=True)
    place_col = away_col[:, 0:1] * rows + rank
    place_row = jnp.broadcast_to(place_col, square).T[0:1, :]
    place_cols = jnp.concatenate([place_col + h * slots for h in range(halves)], axis=0)
    place_rows = jnp.concatenate([place_row + h * slots for h in range(halves)], axis=1)
    spread = onehot(
        iota((n * rows, halves * entries), 0) == place_rows.astype(jnp.int32)
    )
    partner = onehot(iota((n, entries), 0) == away_row[0:1, :].astype(jnp.int32))
    marks = jnp.where(
        iota((entries, LANES), 1) == rank.astype(jnp.int32), wanted + 1.0, 0.0
    ).astype(BF16)
    ids = jnp.dot(partner, marks, preferred_element_type=F32)

    lane = iota((GROUP, width), 1)
    own = (lane // ray_len) == iota((GROUP, width), 0)
    ray = lane % ray_len
    eye = iota((rays_b, rays_b), 0) == iota((rays_b, rays_b), 1)
    count = jnp.sum(
        jnp.where(eye, jnp.broadcast_to(counts_ref[...], (rays_b, rays_b)).astype(F32), 0.0),
        axis=1, keepdims=True,
    ).astype(jnp.int32)

    def repeated(ref, g):
        part = ref[g * GROUP:(g + 1) * GROUP, :]
        return jnp.concatenate([part] * GROUP, axis=1)

    weights, data = [], []
    for g in range(groups):
        prior = repeated(prior_ref, g)
        valid = own & (ray < count[g * GROUP:(g + 1) * GROUP])
        w = jnp.where(valid, jnp.sqrt((FREEDOM + 1.0) / (FREEDOM + prior * prior)), 0.0)
        weights.append(w)
        data.append(w * repeated(times_ref, g))

    def total(parts):
        acc = parts[0] * parts[0]
        for p in parts[1:]:
            acc = acc + p * p
        return jnp.sum(jnp.sum(acc, axis=0, keepdims=True), axis=1, keepdims=True)

    pl.semaphore_wait(barrier, n - 1)

    def exchange(src, dst, size, s_sem, r_sem):
        def part(i):
            i = i * size
            return pl.ds(i if isinstance(i, int) else pl.multiple_of(i, size), size)

        def act(here, there, device):
            pltpu.make_async_remote_copy(
                src_ref=src.at[part(here)], dst_ref=dst.at[part(there)],
                send_sem=s_sem, recv_sem=r_sem, device_id=device, device_id_type=MESH,
            ).start()
        each_partner(act)

    def arrived(dst, size, sem, count=n):
        part = dst.at[pl.ds(size, (count - 1) * size)]
        pltpu.make_async_copy(part, part, sem).wait()

    def send_sum(i, value):
        row = jnp.broadcast_to(value, (1, LANES))
        rad_send[i] = row
        rad_recv[i, 0] = row
        for dr in range(1, n_rad):
            pltpu.make_async_remote_copy(
                src_ref=rad_send.at[i], dst_ref=rad_recv.at[i, n_rad - dr],
                send_sem=rad_send_sem.at[i], recv_sem=rad_recv_sem.at[i],
                device_id=(lat, rads[dr]), device_id_type=MESH,
            ).start()

    def pass_sum(i):
        arrived(rad_recv.at[i], 1, rad_recv_sem.at[i], n_rad)
        row = jnp.sum(rad_recv[i], axis=0)
        lat_send[i] = row
        lat_recv[i, 0] = row

        def act(dl, peer):
            pltpu.make_async_remote_copy(
                src_ref=lat_send.at[i], dst_ref=lat_recv.at[i, n_lat - dl],
                send_sem=lat_send_sem.at[i], recv_sem=lat_recv_sem.at[i],
                device_id=(peer, rad), device_id_type=MESH,
            ).start()
        each_lat(act)

    def get_sum(i):
        arrived(lat_recv.at[i], 1, lat_recv_sem.at[i], n_lat)
        return jnp.sum(lat_recv[i], axis=0)[:, 0:1]

    field4 = (halves, MB_R, MB_L, LANES)
    field = (halves * num_blocks, LANES)
    radial, lateral = halves * MB_L, halves * MB_R
    edge_parts = ((0, radial), (radial, radial), (2 * radial, lateral), (2 * radial + lateral, lateral))
    up = (lat, lax.rem(rad + n_rad - 1, n_rad))
    down = (lat, lax.rem(rad + 1, n_rad))
    left = (lax.rem(lat + n_lat - 1, n_lat), rad)
    right = (lax.rem(lat + 1, n_lat), rad)

    def send_edges(i, x):
        x4 = x.reshape(field4)
        edge_send[i, 0:radial] = x4[:, 0].reshape(radial, LANES)
        edge_send[i, radial:2 * radial] = x4[:, MB_R - 1].reshape(radial, LANES)
        edge_send[i, 2 * radial:2 * radial + lateral] = x4[:, :, 0].reshape(lateral, LANES)
        edge_send[i, 2 * radial + lateral:] = x4[:, :, MB_L - 1].reshape(lateral, LANES)
        for a, b, device in ((0, 1, up), (1, 0, down), (2, 3, left), (3, 2, right)):
            pltpu.make_async_remote_copy(
                src_ref=edge_send.at[i, pl.ds(*edge_parts[a])],
                dst_ref=edge_recv.at[i, pl.ds(*edge_parts[b])],
                send_sem=edge_send_sem.at[i], recv_sem=edge_recv_sem.at[i],
                device_id=device, device_id_type=MESH,
            ).start()

    def roughen(i, x):
        whole = edge_recv.at[i]
        pltpu.make_async_copy(whole, whole, edge_recv_sem.at[i]).wait()

        def edge(part, outside):
            start, size = edge_parts[part]
            return jnp.where(outside, 0.0, edge_recv[i, start:start + size])

        above = edge(0, rad == 0).reshape(halves, 1, MB_L, LANES)
        below = edge(1, rad == n_rad - 1).reshape(halves, 1, MB_L, LANES)
        before = edge(2, lat == 0)
        after = edge(3, lat == n_lat - 1)
        x4 = x.reshape(field4)
        radials = jnp.concatenate([above, x4[:, :-1]], axis=1) + jnp.concatenate(
            [x4[:, 1:], below], axis=1
        )

        def along(e):
            return jnp.broadcast_to(e[:, None, :], (lateral, MB_L, LANES)).reshape(field)

        block_l = iota(field, 0) % MB_L
        prev = jnp.where(block_l == 0, along(before), pltpu.roll(x, 1, 0))
        nxt = jnp.where(block_l == MB_L - 1, along(after), pltpu.roll(x, field[0] - 1, 0))
        return 4.0 * x - (radials.reshape(field) + prev + nxt)

    def tile_part(g, k):
        return tiles[g * GROUP:(g + 1) * GROUP, k].reshape(width, cells)

    def send_rows(i, values):
        send[i] = values.astype(BF16)
        recv[i, 0:rows] = send[i, 0:rows]
        exchange(send.at[i], recv.at[i], rows, send_sem.at[i], recv_sem.at[i])

    def adjoint(i, ray_values, sum_i=None):
        parts = [[None] * groups for _ in range(fanout)]
        for g in range(groups):
            if sum_i is None:
                tile_copy(g).wait()
            y = ray_values[g].astype(BF16)
            for k in range(fanout):
                parts[k][g] = jnp.dot(y, tile_part(g, k), preferred_element_type=F32)
        flat = [p for k in range(fanout) for p in parts[k]]
        stacked = jnp.concatenate(
            [p[:, h * LANES:(h + 1) * LANES] for h in range(halves) for p in flat], axis=0
        ).astype(BF16)
        if sum_i is not None:
            pass_sum(sum_i)
        send_rows(i, jnp.dot(spread, stacked, preferred_element_type=F32))

    def forward(i):
        arrived(recv.at[i], rows, recv_sem.at[i])
        blocks = jnp.dot(pick, recv[i], preferred_element_type=F32)
        out = []
        for g in range(groups):
            acc = None
            for k in range(fanout):
                at_row = k * rays_b + g * GROUP
                v = jnp.concatenate(
                    [
                        blocks[h * entries + at_row:h * entries + at_row + GROUP]
                        for h in range(halves)
                    ],
                    axis=1,
                ).astype(BF16)
                term = lax.dot_general(
                    v, tile_part(g, k), (((1,), (1,)), ((), ())), preferred_element_type=F32
                )
                acc = term if acc is None else acc + term
            out.append(acc)
        return out

    first_sum = total(data)
    id_rows = jnp.where(iota((n, LANES), 1) == slots, first_sum, ids)
    ids_send[...] = id_rows.reshape(n, 1, LANES)
    ids_recv[0] = ids_send[0]
    exchange(ids_send, ids_recv, 1, ids_send_sem, ids_recv_sem)

    adjoint(0, [w * d for w, d in zip(weights, data)])

    pick = onehot(
        iota((halves * entries, n * rows), 1) == place_cols.astype(jnp.int32)
    )

    arrived(ids_recv, 1, ids_recv_sem)
    got = ids_recv[...].reshape(n, LANES)
    beta = jnp.sqrt(jnp.sum(got, axis=0, keepdims=True)[:, slots:slots + 1])
    slot_rows = (n * rows, LANES)
    each = jnp.broadcast_to(got[:, None, :], (n, rows, LANES)).reshape(slot_rows)
    each = jnp.where(iota(slot_rows, 1) == iota(slot_rows, 0) % slots, each, 0.0)
    block_id = jnp.sum(each, axis=1, keepdims=True).astype(jnp.int32)
    asked = jnp.where(iota(slot_rows, 1) + 1 == block_id, 1.0, 0.0)
    half = (iota(slot_rows, 0) % rows) // slots
    served = jnp.concatenate([jnp.where(half == h, asked, 0.0) for h in range(halves)], axis=1)
    gather = served.astype(BF16)
    collect = served.T.astype(BF16)

    def collected(i):
        arrived(recv.at[i], rows, recv_sem.at[i])
        return jnp.dot(collect, recv[i], preferred_element_type=F32)

    x = collected(0) / beta
    data = [d / beta for d in data]
    phi_bar = beta
    round_i, sum_i, edge_i = 1, 0, 0
    pen = search = update = None
    for sweep in range(ITERS):
        send_edges(edge_i, x)
        send_sum(sum_i, total([x]))
        send_rows(round_i, jnp.dot(gather, x.astype(BF16), preferred_element_type=F32))
        pass_sum(sum_i)
        rough = DAMPING * roughen(edge_i, x)
        products = forward(round_i)
        alpha = jnp.sqrt(get_sum(sum_i))
        inverse = 1.0 / alpha
        data = [w * (p * inverse) - alpha * d for w, p, d in zip(weights, products, data)]
        v = x * inverse
        pen_new = inverse * rough
        pen = pen_new if pen is None else pen_new - alpha * pen
        round_i, sum_i, edge_i = round_i + 1, sum_i + 1, edge_i + 1
        if sweep == 0:
            search = v
            rho_bar = alpha
        else:
            search = v - (sine * alpha / rho) * search
            rho_bar = -cosine * alpha
        last = sweep == ITERS - 1
        acc = total(data) + total([pen])
        send_sum(sum_i, acc)
        if not last:
            send_edges(edge_i, pen)
            adjoint(round_i, [w * d for w, d in zip(weights, data)], sum_i)
        else:
            pass_sum(sum_i)
        beta = jnp.sqrt(get_sum(sum_i))
        inverse = 1.0 / beta
        data = [d * inverse for d in data]
        rho = jnp.sqrt(rho_bar * rho_bar + beta * beta)
        cosine, sine = rho_bar / rho, beta / rho
        phi = cosine * phi_bar
        phi_bar = sine * phi_bar
        step = (phi / rho) * search
        update = step if update is None else update + step
        if not last:
            rest = (DAMPING * inverse) * roughen(edge_i, pen) - beta * v
            pen = pen * inverse
            x = collected(round_i) * inverse + rest
            round_i, edge_i = round_i + 1, edge_i + 1
        sum_i += 1

    for h in range(halves):
        part = update[h * num_blocks:(h + 1) * num_blocks]
        update_ref[:, :, h * LANES:(h + 1) * LANES] = part.reshape(MB_R, MB_L, LANES)
    for g in range(groups):
        acc = data[g][:, 0:ray_len]
        for i in range(1, GROUP):
            acc = acc + data[g][:, i * ray_len:(i + 1) * ray_len]
        data_ref[g * GROUP:(g + 1) * GROUP, :] = acc

    def left_buffer(ref, sem):
        pltpu.make_async_copy(ref, ref, sem).wait()

    left_buffer(ids_send.at[pl.ds(1, n - 1)], ids_send_sem)
    for i in range(2 * ITERS):
        left_buffer(send.at[i, pl.ds(rows, (n - 1) * rows)], send_sem.at[i])
    for i in range(2 * ITERS):
        left_buffer(rad_recv.at[i, pl.ds(1, n_rad - 1)], rad_send_sem.at[i])
        left_buffer(lat_recv.at[i, pl.ds(1, n_lat - 1)], lat_send_sem.at[i])
    for i in range(2 * ITERS - 1):
        left_buffer(edge_send.at[i], edge_send_sem.at[i])


def body(kernel, target_device, target_block, counts, traveltimes, prior_residual):
    n_lat, n_rad = lax.axis_size("lat"), lax.axis_size("rad")
    n = n_lat * n_rad
    rays_b, fanout, ray_len, cells = kernel.shape
    capacity = max(2, 2 * rays_b * fanout // n)
    slots = -(-capacity // 8) * 8
    halves = cells // LANES
    rows = halves * slots
    edges = 2 * halves * (MB_R + MB_L)
    payloads, sums, fields = 2 * ITERS, 2 * ITERS, 2 * ITERS - 1
    dma = pltpu.SemaphoreType.DMA
    vmem = pl.BlockSpec(memory_space=pltpu.VMEM)
    operands = (
        kernel, target_device.T, target_block.T, counts.reshape(1, rays_b),
        traveltimes, prior_residual,
    )
    return pl.pallas_call(
        functools.partial(lsqr_kernel, n_lat, n_rad, slots),
        out_shape=(
            jax.ShapeDtypeStruct((MB_R, MB_L, cells), F32),
            jax.ShapeDtypeStruct((rays_b, ray_len), F32),
        ),
        in_specs=[pl.BlockSpec(memory_space=pltpu.HBM)] * len(operands),
        out_specs=(vmem, vmem),
        scratch_shapes=[
            *[pltpu.VMEM(a.shape, a.dtype) for a in operands],
            pltpu.VMEM((payloads, n * rows, LANES), BF16),
            pltpu.VMEM((payloads, n * rows, LANES), BF16),
            pltpu.VMEM((sums, 1, LANES), F32),
            pltpu.VMEM((sums, n_rad, 1, LANES), F32),
            pltpu.VMEM((sums, 1, LANES), F32),
            pltpu.VMEM((sums, n_lat, 1, LANES), F32),
            pltpu.VMEM((fields, edges, LANES), F32),
            pltpu.VMEM((fields, edges, LANES), F32),
            pltpu.VMEM((n, 1, LANES), F32),
            pltpu.VMEM((n, 1, LANES), F32),
            dma((rays_b // GROUP,)),
            dma((len(operands) - 1,)),
            dma((payloads,)), dma((payloads,)),
            dma((sums,)), dma((sums,)), dma((sums,)), dma((sums,)),
            dma((fields,)), dma((fields,)),
            dma, dma,
        ],
        compiler_params=pltpu.CompilerParams(
            collective_id=0, has_side_effects=True, vmem_limit_bytes=64 * 1024 * 1024
        ),
        cost_estimate=pl.CostEstimate(
            flops=14 * kernel.size, bytes_accessed=2 * kernel.size, transcendentals=0
        ),
    )(*operands)


def solution(mesh):
    in_specs = (
        P(("lat", "rad"), None, None, None),
        P(("lat", "rad"), None),
        P(("lat", "rad"), None),
        P(("lat", "rad")),
        P(("lat", "rad"), None),
        P(("lat", "rad"), None),
    )
    out_specs = (P("rad", "lat", None), P(("lat", "rad"), None))
    return jax.shard_map(body, mesh=mesh, in_specs=in_specs, out_specs=out_specs, check_vma=False)
```

```python
import functools

import jax
import jax.numpy as jnp
from jax import lax
from jax.experimental import pallas as pl
from jax.experimental.pallas import tpu as pltpu
from jax.sharding import PartitionSpec as P

ITERS = 3
MB_R = 8
MB_L = 16
FREEDOM = 4.0
DAMPING = 0.3
LANES = 128
GROUP = 8

F32 = jnp.float32
BF16 = jnp.bfloat16
MESH = pl.DeviceIdType.MESH


def iota(shape, dim):
    return lax.broadcasted_iota(jnp.int32, shape, dim)


def onehot(cond):
    return jnp.where(cond, 1.0, 0.0).astype(BF16)


def lsqr_kernel(
    n_lat, n_rad, slots,
    kernel_ref, target_hbm, block_hbm, counts_hbm, times_hbm, prior_hbm,
    update_ref, data_ref,
    tiles, target_ref, block_ref, counts_ref, times_ref, prior_ref,
    send, recv, rad_send, rad_recv, lat_send, lat_recv,
    edge_send, edge_recv, ids_send, ids_recv,
    tile_sem, small_sem, send_sem, recv_sem, rad_send_sem, rad_recv_sem,
    lat_send_sem, lat_recv_sem, edge_send_sem, edge_recv_sem, ids_send_sem, ids_recv_sem,
):
    n = n_lat * n_rad
    rays_b, fanout, ray_len, cells = tiles.shape
    entries = rays_b * fanout
    halves = cells // LANES
    rows = halves * slots
    num_blocks = MB_R * MB_L
    groups = rays_b // GROUP
    width = GROUP * ray_len
    lat, rad = lax.axis_index("lat"), lax.axis_index("rad")

    small = (
        (target_hbm, target_ref), (block_hbm, block_ref), (counts_hbm, counts_ref),
        (times_hbm, times_ref), (prior_hbm, prior_ref),
    )
    for i, (src, dst) in enumerate(small):
        pltpu.make_async_copy(src, dst, small_sem.at[i]).start()

    def tile_copy(g):
        part = pl.ds(g * GROUP, GROUP)
        return pltpu.make_async_copy(kernel_ref.at[part], tiles.at[part], tile_sem.at[g])

    for g in range(groups):
        tile_copy(g).start()

    rads = [lax.rem(rad + dr, n_rad) for dr in range(n_rad)]

    def each_lat(act):
        def go(i, carry):
            dl = n_lat // 2 + (2 * lax.rem(i, 2) - 1) * ((i + 1) // 2)
            act(dl, lax.rem(lat + dl, n_lat))
            return carry
        lax.fori_loop(0, n_lat - 1, go, 0)

    def each_partner(act):
        def row(dl, peer):
            here, there = dl * n_rad, (n_lat - dl) * n_rad
            for dr in range(n_rad):
                act(here + dr, there + (n_rad - dr) % n_rad, (peer, rads[dr]))
        each_lat(row)
        for dr in range(1, n_rad):
            act(dr, n_rad - dr, (lat, rads[dr]))

    barrier = pltpu.get_barrier_semaphore()
    each_partner(
        lambda here, there, device: pl.semaphore_signal(
            barrier, inc=1, device_id=device, device_id_type=MESH
        )
    )
    for i, (src, dst) in enumerate(small):
        pltpu.make_async_copy(src, dst, small_sem.at[i]).wait()

    square = (entries, entries)
    named = jnp.concatenate([target_ref[k:k + 1, :] for k in range(fanout)], axis=1)
    wanted = jnp.concatenate([block_ref[k:k + 1, :] for k in range(fanout)], axis=1)
    away_lat = named // n_rad - lat
    away_rad = named % n_rad - rad
    away_lat = jnp.where(away_lat < 0, away_lat + n_lat, away_lat)
    away_rad = jnp.where(away_rad < 0, away_rad + n_rad, away_rad)
    away_row = jnp.broadcast_to((away_lat * n_rad + away_rad).astype(F32), square)
    away_col = away_row.T
    wanted = jnp.broadcast_to(wanted.astype(F32), square).T[:, 0:1]
    earlier = (away_col == away_row) & (iota(square, 1) < iota(square, 0))
    rank = jnp.sum(jnp.where(earlier, 1.0, 0.0), axis=1, keepdims=True)
    place_col = away_col[:, 0:1] * rows + rank
    place_row = jnp.broadcast_to(place_col, square).T[0:1, :]
    place_cols = jnp.concatenate([place_col + h * slots for h in range(halves)], axis=0)
    place_rows = jnp.concatenate([place_row + h * slots for h in range(halves)], axis=1)
    spread = onehot(
        iota((n * rows, halves * entries), 0) == place_rows.astype(jnp.int32)
    )
    partner = onehot(iota((n, entries), 0) == away_row[0:1, :].astype(jnp.int32))
    marks = jnp.where(
        iota((entries, LANES), 1) == rank.astype(jnp.int32), wanted + 1.0, 0.0
    ).astype(BF16)
    ids = jnp.dot(partner, marks, preferred_element_type=F32)

    lane = iota((GROUP, width), 1)
    own = (lane // ray_len) == iota((GROUP, width), 0)
    ray = lane % ray_len
    eye = iota((rays_b, rays_b), 0) == iota((rays_b, rays_b), 1)
    count = jnp.sum(
        jnp.where(eye, jnp.broadcast_to(counts_ref[...], (rays_b, rays_b)).astype(F32), 0.0),
        axis=1, keepdims=True,
    ).astype(jnp.int32)

    def repeated(ref, g):
        part = ref[g * GROUP:(g + 1) * GROUP, :]
        return jnp.concatenate([part] * GROUP, axis=1)

    weights, data = [], []
    for g in range(groups):
        prior = repeated(prior_ref, g)
        valid = own & (ray < count[g * GROUP:(g + 1) * GROUP])
        w = jnp.where(valid, jnp.sqrt((FREEDOM + 1.0) / (FREEDOM + prior * prior)), 0.0)
        weights.append(w)
        data.append(w * repeated(times_ref, g))

    def total(parts):
        acc = parts[0] * parts[0]
        for p in parts[1:]:
            acc = acc + p * p
        return jnp.sum(jnp.sum(acc, axis=0, keepdims=True), axis=1, keepdims=True)

    pl.semaphore_wait(barrier, n - 1)

    def exchange(src, dst, size, s_sem, r_sem):
        def part(i):
            i = i * size
            return pl.ds(i if isinstance(i, int) else pl.multiple_of(i, size), size)

        def act(here, there, device):
            pltpu.make_async_remote_copy(
                src_ref=src.at[part(here)], dst_ref=dst.at[part(there)],
                send_sem=s_sem, recv_sem=r_sem, device_id=device, device_id_type=MESH,
            ).start()
        each_partner(act)

    def arrived(dst, size, sem, count=n):
        part = dst.at[pl.ds(size, (count - 1) * size)]
        pltpu.make_async_copy(part, part, sem).wait()

    def send_sum(i, value):
        row = jnp.broadcast_to(value, (1, LANES))
        rad_send[i] = row
        rad_recv[i, 0] = row
        for dr in range(1, n_rad):
            pltpu.make_async_remote_copy(
                src_ref=rad_send.at[i], dst_ref=rad_recv.at[i, n_rad - dr],
                send_sem=rad_send_sem.at[i], recv_sem=rad_recv_sem.at[i],
                device_id=(lat, rads[dr]), device_id_type=MESH,
            ).start()

    def pass_sum(i):
        arrived(rad_recv.at[i], 1, rad_recv_sem.at[i], n_rad)
        row = jnp.sum(rad_recv[i], axis=0)
        lat_send[i] = row
        lat_recv[i, 0] = row

        def act(dl, peer):
            pltpu.make_async_remote_copy(
                src_ref=lat_send.at[i], dst_ref=lat_recv.at[i, n_lat - dl],
                send_sem=lat_send_sem.at[i], recv_sem=lat_recv_sem.at[i],
                device_id=(peer, rad), device_id_type=MESH,
            ).start()
        each_lat(act)

    def get_sum(i):
        arrived(lat_recv.at[i], 1, lat_recv_sem.at[i], n_lat)
        return jnp.sum(lat_recv[i], axis=0)[:, 0:1]

    field4 = (halves, MB_R, MB_L, LANES)
    field = (halves * num_blocks, LANES)
    radial, lateral = halves * MB_L, halves * MB_R
    edge_parts = ((0, radial), (radial, radial), (2 * radial, lateral), (2 * radial + lateral, lateral))
    up = (lat, lax.rem(rad + n_rad - 1, n_rad))
    down = (lat, lax.rem(rad + 1, n_rad))
    left = (lax.rem(lat + n_lat - 1, n_lat), rad)
    right = (lax.rem(lat + 1, n_lat), rad)

    def send_edges(i, x):
        x4 = x.reshape(field4)
        edge_send[i, 0:radial] = x4[:, 0].reshape(radial, LANES)
        edge_send[i, radial:2 * radial] = x4[:, MB_R - 1].reshape(radial, LANES)
        edge_send[i, 2 * radial:2 * radial + lateral] = x4[:, :, 0].reshape(lateral, LANES)
        edge_send[i, 2 * radial + lateral:] = x4[:, :, MB_L - 1].reshape(lateral, LANES)
        for a, b, device in ((0, 1, up), (1, 0, down), (2, 3, left), (3, 2, right)):
            pltpu.make_async_remote_copy(
                src_ref=edge_send.at[i, pl.ds(*edge_parts[a])],
                dst_ref=edge_recv.at[i, pl.ds(*edge_parts[b])],
                send_sem=edge_send_sem.at[i], recv_sem=edge_recv_sem.at[i],
                device_id=device, device_id_type=MESH,
            ).start()

    def roughen(i, x):
        whole = edge_recv.at[i]
        pltpu.make_async_copy(whole, whole, edge_recv_sem.at[i]).wait()

        def edge(part, outside):
            start, size = edge_parts[part]
            return jnp.where(outside, 0.0, edge_recv[i, start:start + size])

        above = edge(0, rad == 0).reshape(halves, 1, MB_L, LANES)
        below = edge(1, rad == n_rad - 1).reshape(halves, 1, MB_L, LANES)
        before = edge(2, lat == 0)
        after = edge(3, lat == n_lat - 1)
        x4 = x.reshape(field4)
        radials = jnp.concatenate([above, x4[:, :-1]], axis=1) + jnp.concatenate(
            [x4[:, 1:], below], axis=1
        )

        def along(e):
            return jnp.broadcast_to(e[:, None, :], (lateral, MB_L, LANES)).reshape(field)

        block_l = iota(field, 0) % MB_L
        prev = jnp.where(block_l == 0, along(before), pltpu.roll(x, 1, 0))
        nxt = jnp.where(block_l == MB_L - 1, along(after), pltpu.roll(x, field[0] - 1, 0))
        return 4.0 * x - (radials.reshape(field) + prev + nxt)

    def tile_part(g, k):
        return tiles[g * GROUP:(g + 1) * GROUP, k].reshape(width, cells)

    def send_rows(i, values):
        send[i] = values.astype(BF16)
        recv[i, 0:rows] = send[i, 0:rows]
        exchange(send.at[i], recv.at[i], rows, send_sem.at[i], recv_sem.at[i])

    def adjoint(i, ray_values, sum_i=None):
        parts = [[None] * groups for _ in range(fanout)]
        for g in range(groups):
            if sum_i is None:
                tile_copy(g).wait()
            y = ray_values[g].astype(BF16)
            for k in range(fanout):
                parts[k][g] = jnp.dot(y, tile_part(g, k), preferred_element_type=F32)
        flat = [p for k in range(fanout) for p in parts[k]]
        stacked = jnp.concatenate(
            [p[:, h * LANES:(h + 1) * LANES] for h in range(halves) for p in flat], axis=0
        ).astype(BF16)
        if sum_i is not None:
            pass_sum(sum_i)
        send_rows(i, jnp.dot(spread, stacked, preferred_element_type=F32))

    def forward(i):
        arrived(recv.at[i], rows, recv_sem.at[i])
        blocks = jnp.dot(pick, recv[i], preferred_element_type=F32)
        turned = jnp.concatenate(
            [blocks[h * entries:(h + 1) * entries].T for h in range(halves)], axis=0
        )
        columns = [
            (pltpu.roll(turned, entries - k * rays_b, 1) if k else turned).astype(BF16)
            for k in range(fanout)
        ]
        out = []
        for g in range(groups):
            acc = None
            for k in range(fanout):
                term = jnp.dot(tile_part(g, k), columns[k], preferred_element_type=F32)
                acc = term if acc is None else acc + term
            out.append(acc.T[g * GROUP:(g + 1) * GROUP, :])
        return out

    first_sum = total(data)
    id_rows = jnp.where(iota((n, LANES), 1) == slots, first_sum, ids)
    ids_send[...] = id_rows.reshape(n, 1, LANES)
    ids_recv[0] = ids_send[0]
    exchange(ids_send, ids_recv, 1, ids_send_sem, ids_recv_sem)

    adjoint(0, [w * d for w, d in zip(weights, data)])

    pick = onehot(
        iota((halves * entries, n * rows), 1) == place_cols.astype(jnp.int32)
    )

    arrived(ids_recv, 1, ids_recv_sem)
    got = ids_recv[...].reshape(n, LANES)
    beta = jnp.sqrt(jnp.sum(got, axis=0, keepdims=True)[:, slots:slots + 1])
    slot_rows = (n * rows, LANES)
    each = jnp.broadcast_to(got[:, None, :], (n, rows, LANES)).reshape(slot_rows)
    each = jnp.where(iota(slot_rows, 1) == iota(slot_rows, 0) % slots, each, 0.0)
    block_id = jnp.sum(each, axis=1, keepdims=True).astype(jnp.int32)
    asked = jnp.where(iota(slot_rows, 1) + 1 == block_id, 1.0, 0.0)
    half = (iota(slot_rows, 0) % rows) // slots
    served = jnp.concatenate([jnp.where(half == h, asked, 0.0) for h in range(halves)], axis=1)
    gather = served.astype(BF16)
    collect = served.T.astype(BF16)

    def collected(i):
        arrived(recv.at[i], rows, recv_sem.at[i])
        return jnp.dot(collect, recv[i], preferred_element_type=F32)

    x = collected(0) / beta
    data = [d / beta for d in data]
    phi_bar = beta
    round_i, sum_i, edge_i = 1, 0, 0
    pen = search = update = None
    for sweep in range(ITERS):
        send_edges(edge_i, x)
        send_sum(sum_i, total([x]))
        send_rows(round_i, jnp.dot(gather, x.astype(BF16), preferred_element_type=F32))
        pass_sum(sum_i)
        rough = DAMPING * roughen(edge_i, x)
        products = forward(round_i)
        alpha = jnp.sqrt(get_sum(sum_i))
        inverse = 1.0 / alpha
        data = [w * (p * inverse) - alpha * d for w, p, d in zip(weights, products, data)]
        v = x * inverse
        pen_new = inverse * rough
        pen = pen_new if pen is None else pen_new - alpha * pen
        round_i, sum_i, edge_i = round_i + 1, sum_i + 1, edge_i + 1
        if sweep == 0:
            search = v
            rho_bar = alpha
        else:
            search = v - (sine * alpha / rho) * search
            rho_bar = -cosine * alpha
        last = sweep == ITERS - 1
        acc = total(data) + total([pen])
        send_sum(sum_i, acc)
        if not last:
            send_edges(edge_i, pen)
            adjoint(round_i, [w * d for w, d in zip(weights, data)], sum_i)
        else:
            pass_sum(sum_i)
        beta = jnp.sqrt(get_sum(sum_i))
        inverse = 1.0 / beta
        data = [d * inverse for d in data]
        rho = jnp.sqrt(rho_bar * rho_bar + beta * beta)
        cosine, sine = rho_bar / rho, beta / rho
        phi = cosine * phi_bar
        phi_bar = sine * phi_bar
        step = (phi / rho) * search
        update = step if update is None else update + step
        if not last:
            rest = (DAMPING * inverse) * roughen(edge_i, pen) - beta * v
            pen = pen * inverse
            x = collected(round_i) * inverse + rest
            round_i, edge_i = round_i + 1, edge_i + 1
        sum_i += 1

    for h in range(halves):
        part = update[h * num_blocks:(h + 1) * num_blocks]
        update_ref[:, :, h * LANES:(h + 1) * LANES] = part.reshape(MB_R, MB_L, LANES)
    for g in range(groups):
        acc = data[g][:, 0:ray_len]
        for i in range(1, GROUP):
            acc = acc + data[g][:, i * ray_len:(i + 1) * ray_len]
        data_ref[g * GROUP:(g + 1) * GROUP, :] = acc

    def left_buffer(ref, sem):
        pltpu.make_async_copy(ref, ref, sem).wait()

    left_buffer(ids_send.at[pl.ds(1, n - 1)], ids_send_sem)
    for i in range(2 * ITERS):
        left_buffer(send.at[i, pl.ds(rows, (n - 1) * rows)], send_sem.at[i])
    for i in range(2 * ITERS):
        left_buffer(rad_recv.at[i, pl.ds(1, n_rad - 1)], rad_send_sem.at[i])
        left_buffer(lat_recv.at[i, pl.ds(1, n_lat - 1)], lat_send_sem.at[i])
    for i in range(2 * ITERS - 1):
        left_buffer(edge_send.at[i], edge_send_sem.at[i])


def body(kernel, target_device, target_block, counts, traveltimes, prior_residual):
    n_lat, n_rad = lax.axis_size("lat"), lax.axis_size("rad")
    n = n_lat * n_rad
    rays_b, fanout, ray_len, cells = kernel.shape
    capacity = max(2, 2 * rays_b * fanout // n)
    slots = -(-capacity // 8) * 8
    halves = cells // LANES
    rows = halves * slots
    edges = 2 * halves * (MB_R + MB_L)
    payloads, sums, fields = 2 * ITERS, 2 * ITERS, 2 * ITERS - 1
    dma = pltpu.SemaphoreType.DMA
    vmem = pl.BlockSpec(memory_space=pltpu.VMEM)
    operands = (
        kernel, target_device.T, target_block.T, counts.reshape(1, rays_b),
        traveltimes, prior_residual,
    )
    return pl.pallas_call(
        functools.partial(lsqr_kernel, n_lat, n_rad, slots),
        out_shape=(
            jax.ShapeDtypeStruct((MB_R, MB_L, cells), F32),
            jax.ShapeDtypeStruct((rays_b, ray_len), F32),
        ),
        in_specs=[pl.BlockSpec(memory_space=pltpu.HBM)] * len(operands),
        out_specs=(vmem, vmem),
        scratch_shapes=[
            *[pltpu.VMEM(a.shape, a.dtype) for a in operands],
            pltpu.VMEM((payloads, n * rows, LANES), BF16),
            pltpu.VMEM((payloads, n * rows, LANES), BF16),
            pltpu.VMEM((sums, 1, LANES), F32),
            pltpu.VMEM((sums, n_rad, 1, LANES), F32),
            pltpu.VMEM((sums, 1, LANES), F32),
            pltpu.VMEM((sums, n_lat, 1, LANES), F32),
            pltpu.VMEM((fields, edges, LANES), F32),
            pltpu.VMEM((fields, edges, LANES), F32),
            pltpu.VMEM((n, 1, LANES), F32),
            pltpu.VMEM((n, 1, LANES), F32),
            dma((rays_b // GROUP,)),
            dma((len(operands) - 1,)),
            dma((payloads,)), dma((payloads,)),
            dma((sums,)), dma((sums,)), dma((sums,)), dma((sums,)),
            dma((fields,)), dma((fields,)),
            dma, dma,
        ],
        compiler_params=pltpu.CompilerParams(
            collective_id=0, has_side_effects=True, vmem_limit_bytes=64 * 1024 * 1024
        ),
        cost_estimate=pl.CostEstimate(
            flops=14 * kernel.size, bytes_accessed=2 * kernel.size, transcendentals=0
        ),
    )(*operands)


def solution(mesh):
    in_specs = (
        P(("lat", "rad"), None, None, None),
        P(("lat", "rad"), None),
        P(("lat", "rad"), None),
        P(("lat", "rad")),
        P(("lat", "rad"), None),
        P(("lat", "rad"), None),
    )
    out_specs = (P("rad", "lat", None), P(("lat", "rad"), None))
    return jax.shard_map(body, mesh=mesh, in_specs=in_specs, out_specs=out_specs, check_vma=False)
```

```python
import functools

import jax
import jax.numpy as jnp
from jax import lax
from jax.experimental import pallas as pl
from jax.experimental.pallas import tpu as pltpu
from jax.sharding import PartitionSpec as P

ITERS = 3
MB_R = 8
MB_L = 16
FREEDOM = 4.0
DAMPING = 0.3
LANES = 128
GROUP = 8

F32 = jnp.float32
BF16 = jnp.bfloat16
MESH = pl.DeviceIdType.MESH


def iota(shape, dim):
    return lax.broadcasted_iota(jnp.int32, shape, dim)


def onehot(cond):
    return jnp.where(cond, 1.0, 0.0).astype(BF16)


def lsqr_kernel(
    n_lat, n_rad, slots,
    kernel_ref, target_hbm, block_hbm, counts_hbm, times_hbm, prior_hbm,
    update_ref, data_ref,
    tiles, target_ref, block_ref, counts_ref, times_ref, prior_ref,
    send, recv, rad_send, rad_recv, lat_send, lat_recv,
    edge_send, edge_recv, ids_send, ids_recv,
    tile_sem, small_sem, send_sem, recv_sem, rad_send_sem, rad_recv_sem,
    lat_send_sem, lat_recv_sem, edge_send_sem, edge_recv_sem, ids_send_sem, ids_recv_sem,
):
    n = n_lat * n_rad
    rays_b, fanout, ray_len, cells = tiles.shape
    entries = rays_b * fanout
    halves = cells // LANES
    rows = halves * slots
    num_blocks = MB_R * MB_L
    groups = rays_b // GROUP
    width = GROUP * ray_len
    lat, rad = lax.axis_index("lat"), lax.axis_index("rad")

    small = (
        (target_hbm, target_ref), (block_hbm, block_ref), (counts_hbm, counts_ref),
        (times_hbm, times_ref), (prior_hbm, prior_ref),
    )
    for i, (src, dst) in enumerate(small):
        pltpu.make_async_copy(src, dst, small_sem.at[i]).start()

    def tile_copy(g):
        part = pl.ds(g * GROUP, GROUP)
        return pltpu.make_async_copy(kernel_ref.at[part], tiles.at[part], tile_sem.at[g])

    for g in range(groups):
        tile_copy(g).start()

    rads = [lax.rem(rad + dr, n_rad) for dr in range(n_rad)]

    def each_lat(act):
        def go(dl, carry):
            act(dl, lax.rem(lat + dl, n_lat))
            return carry
        lax.fori_loop(1, n_lat, go, 0)

    def each_partner(act):
        for dr in range(1, n_rad):
            act(dr, n_rad - dr, (lat, rads[dr]))

        def row(dl, peer):
            here, there = dl * n_rad, (n_lat - dl) * n_rad
            for dr in range(n_rad):
                act(here + dr, there + (n_rad - dr) % n_rad, (peer, rads[dr]))
        each_lat(row)

    barrier = pltpu.get_barrier_semaphore()
    each_partner(
        lambda here, there, device: pl.semaphore_signal(
            barrier, inc=1, device_id=device, device_id_type=MESH
        )
    )
    for i, (src, dst) in enumerate(small):
        pltpu.make_async_copy(src, dst, small_sem.at[i]).wait()

    square = (entries, entries)
    named = jnp.concatenate([target_ref[k:k + 1, :] for k in range(fanout)], axis=1)
    wanted = jnp.concatenate([block_ref[k:k + 1, :] for k in range(fanout)], axis=1)
    away_lat = named // n_rad - lat
    away_rad = named % n_rad - rad
    away_lat = jnp.where(away_lat < 0, away_lat + n_lat, away_lat)
    away_rad = jnp.where(away_rad < 0, away_rad + n_rad, away_rad)
    away_row = jnp.broadcast_to((away_lat * n_rad + away_rad).astype(F32), square)
    away_col = away_row.T
    wanted = jnp.broadcast_to(wanted.astype(F32), square).T[:, 0:1]
    earlier = (away_col == away_row) & (iota(square, 1) < iota(square, 0))
    rank = jnp.sum(jnp.where(earlier, 1.0, 0.0), axis=1, keepdims=True)
    place_col = away_col[:, 0:1] * rows + rank
    place_row = jnp.broadcast_to(place_col, square).T[0:1, :]
    place_cols = jnp.concatenate([place_col + h * slots for h in range(halves)], axis=0)
    place_rows = jnp.concatenate([place_row + h * slots for h in range(halves)], axis=1)
    spread = onehot(
        iota((n * rows, halves * entries), 0) == place_rows.astype(jnp.int32)
    )
    partner = onehot(iota((n, entries), 0) == away_row[0:1, :].astype(jnp.int32))
    marks = jnp.where(
        iota((entries, LANES), 1) == rank.astype(jnp.int32), wanted + 1.0, 0.0
    ).astype(BF16)
    ids = jnp.dot(partner, marks, preferred_element_type=F32)

    lane = iota((GROUP, width), 1)
    own = (lane // ray_len) == iota((GROUP, width), 0)
    ray = lane % ray_len
    eye = iota((rays_b, rays_b), 0) == iota((rays_b, rays_b), 1)
    count = jnp.sum(
        jnp.where(eye, jnp.broadcast_to(counts_ref[...], (rays_b, rays_b)).astype(F32), 0.0),
        axis=1, keepdims=True,
    ).astype(jnp.int32)

    def repeated(ref, g):
        part = ref[g * GROUP:(g + 1) * GROUP, :]
        return jnp.concatenate([part] * GROUP, axis=1)

    weights, data = [], []
    for g in range(groups):
        prior = repeated(prior_ref, g)
        valid = own & (ray < count[g * GROUP:(g + 1) * GROUP])
        w = jnp.where(valid, jnp.sqrt((FREEDOM + 1.0) / (FREEDOM + prior * prior)), 0.0)
        weights.append(w)
        data.append(w * repeated(times_ref, g))

    def total(parts):
        acc = parts[0] * parts[0]
        for p in parts[1:]:
            acc = acc + p * p
        return jnp.sum(jnp.sum(acc, axis=0, keepdims=True), axis=1, keepdims=True)

    pl.semaphore_wait(barrier, n - 1)

    def exchange(src, dst, size, s_sem, r_sem):
        def part(i):
            i = i * size
            return pl.ds(i if isinstance(i, int) else pl.multiple_of(i, size), size)

        def act(here, there, device):
            pltpu.make_async_remote_copy(
                src_ref=src.at[part(here)], dst_ref=dst.at[part(there)],
                send_sem=s_sem, recv_sem=r_sem, device_id=device, device_id_type=MESH,
            ).start()
        each_partner(act)

    def arrived(dst, size, sem, count=n):
        part = dst.at[pl.ds(size, (count - 1) * size)]
        pltpu.make_async_copy(part, part, sem).wait()

    def send_sum(i, value):
        row = jnp.broadcast_to(value, (1, LANES))
        rad_send[i] = row
        rad_recv[i, 0] = row
        for dr in range(1, n_rad):
            pltpu.make_async_remote_copy(
                src_ref=rad_send.at[i], dst_ref=rad_recv.at[i, n_rad - dr],
                send_sem=rad_send_sem.at[i], recv_sem=rad_recv_sem.at[i],
                device_id=(lat, rads[dr]), device_id_type=MESH,
            ).start()

    def pass_sum(i):
        arrived(rad_recv.at[i], 1, rad_recv_sem.at[i], n_rad)
        row = jnp.sum(rad_recv[i], axis=0)
        lat_send[i] = row
        lat_recv[i, 0] = row

        def act(dl, peer):
            pltpu.make_async_remote_copy(
                src_ref=lat_send.at[i], dst_ref=lat_recv.at[i, n_lat - dl],
                send_sem=lat_send_sem.at[i], recv_sem=lat_recv_sem.at[i],
                device_id=(peer, rad), device_id_type=MESH,
            ).start()
        each_lat(act)

    def get_sum(i):
        arrived(lat_recv.at[i], 1, lat_recv_sem.at[i], n_lat)
        return jnp.sum(lat_recv[i], axis=0)[:, 0:1]

    field4 = (halves, MB_R, MB_L, LANES)
    field = (halves * num_blocks, LANES)
    radial, lateral = halves * MB_L, halves * MB_R
    edge_parts = ((0, radial), (radial, radial), (2 * radial, lateral), (2 * radial + lateral, lateral))
    up = (lat, lax.rem(rad + n_rad - 1, n_rad))
    down = (lat, lax.rem(rad + 1, n_rad))
    left = (lax.rem(lat + n_lat - 1, n_lat), rad)
    right = (lax.rem(lat + 1, n_lat), rad)

    def send_edges(i, x):
        x4 = x.reshape(field4)
        edge_send[i, 0:radial] = x4[:, 0].reshape(radial, LANES)
        edge_send[i, radial:2 * radial] = x4[:, MB_R - 1].reshape(radial, LANES)
        edge_send[i, 2 * radial:2 * radial + lateral] = x4[:, :, 0].reshape(lateral, LANES)
        edge_send[i, 2 * radial + lateral:] = x4[:, :, MB_L - 1].reshape(lateral, LANES)
        for a, b, device in ((0, 1, up), (1, 0, down), (2, 3, left), (3, 2, right)):
            pltpu.make_async_remote_copy(
                src_ref=edge_send.at[i, pl.ds(*edge_parts[a])],
                dst_ref=edge_recv.at[i, pl.ds(*edge_parts[b])],
                send_sem=edge_send_sem.at[i], recv_sem=edge_recv_sem.at[i],
                device_id=device, device_id_type=MESH,
            ).start()

    def roughen(i, x):
        whole = edge_recv.at[i]
        pltpu.make_async_copy(whole, whole, edge_recv_sem.at[i]).wait()

        def edge(part, outside):
            start, size = edge_parts[part]
            return jnp.where(outside, 0.0, edge_recv[i, start:start + size])

        above = edge(0, rad == 0).reshape(halves, 1, MB_L, LANES)
        below = edge(1, rad == n_rad - 1).reshape(halves, 1, MB_L, LANES)
        before = edge(2, lat == 0)
        after = edge(3, lat == n_lat - 1)
        x4 = x.reshape(field4)
        radials = jnp.concatenate([above, x4[:, :-1]], axis=1) + jnp.concatenate(
            [x4[:, 1:], below], axis=1
        )

        def along(e):
            return jnp.broadcast_to(e[:, None, :], (lateral, MB_L, LANES)).reshape(field)

        block_l = iota(field, 0) % MB_L
        prev = jnp.where(block_l == 0, along(before), pltpu.roll(x, 1, 0))
        nxt = jnp.where(block_l == MB_L - 1, along(after), pltpu.roll(x, field[0] - 1, 0))
        return 4.0 * x - (radials.reshape(field) + prev + nxt)

    def tile_part(g, k):
        return tiles[g * GROUP:(g + 1) * GROUP, k].reshape(width, cells)

    def send_rows(i, values):
        send[i] = values.astype(BF16)
        recv[i, 0:rows] = send[i, 0:rows]
        exchange(send.at[i], recv.at[i], rows, send_sem.at[i], recv_sem.at[i])

    def adjoint(i, ray_values, sum_i=None):
        parts = [[None] * groups for _ in range(fanout)]
        for g in range(groups):
            if sum_i is None:
                tile_copy(g).wait()
            y = ray_values[g].astype(BF16)
            for k in range(fanout):
                parts[k][g] = jnp.dot(y, tile_part(g, k), preferred_element_type=F32)
        flat = [p for k in range(fanout) for p in parts[k]]
        stacked = jnp.concatenate(
            [p[:, h * LANES:(h + 1) * LANES] for h in range(halves) for p in flat], axis=0
        ).astype(BF16)
        if sum_i is not None:
            pass_sum(sum_i)
        send_rows(i, jnp.dot(spread, stacked, preferred_element_type=F32))

    def forward(i):
        arrived(recv.at[i], rows, recv_sem.at[i])
        blocks = jnp.dot(pick, recv[i], preferred_element_type=F32)
        out = []
        for g in range(groups):
            acc = None
            for k in range(fanout):
                at_row = k * rays_b + g * GROUP
                v = jnp.concatenate(
                    [
                        blocks[h * entries + at_row:h * entries + at_row + GROUP]
                        for h in range(halves)
                    ],
                    axis=1,
                ).astype(BF16)
                term = lax.dot_general(
                    v, tile_part(g, k), (((1,), (1,)), ((), ())), preferred_element_type=F32
                )
                acc = term if acc is None else acc + term
            out.append(acc)
        return out

    first_sum = total(data)
    id_rows = jnp.where(iota((n, LANES), 1) == slots, first_sum, ids)
    ids_send[...] = id_rows.reshape(n, 1, LANES)
    ids_recv[0] = ids_send[0]
    exchange(ids_send, ids_recv, 1, ids_send_sem, ids_recv_sem)

    adjoint(0, [w * d for w, d in zip(weights, data)])

    pick = onehot(
        iota((halves * entries, n * rows), 1) == place_cols.astype(jnp.int32)
    )

    arrived(ids_recv, 1, ids_recv_sem)
    got = ids_recv[...].reshape(n, LANES)
    beta = jnp.sqrt(jnp.sum(got, axis=0, keepdims=True)[:, slots:slots + 1])
    slot_rows = (n * rows, LANES)
    each = jnp.broadcast_to(got[:, None, :], (n, rows, LANES)).reshape(slot_rows)
    each = jnp.where(iota(slot_rows, 1) == iota(slot_rows, 0) % slots, each, 0.0)
    block_id = jnp.sum(each, axis=1, keepdims=True).astype(jnp.int32)
    asked = jnp.where(iota(slot_rows, 1) + 1 == block_id, 1.0, 0.0)
    half = (iota(slot_rows, 0) % rows) // slots
    served = jnp.concatenate([jnp.where(half == h, asked, 0.0) for h in range(halves)], axis=1)
    gather = served.astype(BF16)
    collect = served.T.astype(BF16)

    def collected(i):
        arrived(recv.at[i], rows, recv_sem.at[i])
        return jnp.dot(collect, recv[i], preferred_element_type=F32)

    x = collected(0) / beta
    data = [d / beta for d in data]
    phi_bar = beta
    round_i, sum_i, edge_i = 1, 0, 0
    pen = search = update = None
    for sweep in range(ITERS):
        send_rows(round_i, jnp.dot(gather, x.astype(BF16), preferred_element_type=F32))
        send_sum(sum_i, total([x]))
        send_edges(edge_i, x)
        pass_sum(sum_i)
        rough = DAMPING * roughen(edge_i, x)
        products = forward(round_i)
        alpha = jnp.sqrt(get_sum(sum_i))
        inverse = 1.0 / alpha
        data = [w * (p * inverse) - alpha * d for w, p, d in zip(weights, products, data)]
        v = x * inverse
        pen_new = inverse * rough
        pen = pen_new if pen is None else pen_new - alpha * pen
        round_i, sum_i, edge_i = round_i + 1, sum_i + 1, edge_i + 1
        if sweep == 0:
            search = v
            rho_bar = alpha
        else:
            search = v - (sine * alpha / rho) * search
            rho_bar = -cosine * alpha
        last = sweep == ITERS - 1
        acc = total(data) + total([pen])
        send_sum(sum_i, acc)
        if not last:
            send_edges(edge_i, pen)
            adjoint(round_i, [w * d for w, d in zip(weights, data)], sum_i)
        else:
            pass_sum(sum_i)
        beta = jnp.sqrt(get_sum(sum_i))
        inverse = 1.0 / beta
        data = [d * inverse for d in data]
        rho = jnp.sqrt(rho_bar * rho_bar + beta * beta)
        cosine, sine = rho_bar / rho, beta / rho
        phi = cosine * phi_bar
        phi_bar = sine * phi_bar
        step = (phi / rho) * search
        update = step if update is None else update + step
        if not last:
            rest = (DAMPING * inverse) * roughen(edge_i, pen) - beta * v
            pen = pen * inverse
            x = collected(round_i) * inverse + rest
            round_i, edge_i = round_i + 1, edge_i + 1
        sum_i += 1

    for h in range(halves):
        part = update[h * num_blocks:(h + 1) * num_blocks]
        update_ref[:, :, h * LANES:(h + 1) * LANES] = part.reshape(MB_R, MB_L, LANES)
    for g in range(groups):
        acc = data[g][:, 0:ray_len]
        for i in range(1, GROUP):
            acc = acc + data[g][:, i * ray_len:(i + 1) * ray_len]
        data_ref[g * GROUP:(g + 1) * GROUP, :] = acc

    def left_buffer(ref, sem):
        pltpu.make_async_copy(ref, ref, sem).wait()

    left_buffer(ids_send.at[pl.ds(1, n - 1)], ids_send_sem)
    for i in range(2 * ITERS):
        left_buffer(send.at[i, pl.ds(rows, (n - 1) * rows)], send_sem.at[i])
    for i in range(2 * ITERS):
        left_buffer(rad_recv.at[i, pl.ds(1, n_rad - 1)], rad_send_sem.at[i])
        left_buffer(lat_recv.at[i, pl.ds(1, n_lat - 1)], lat_send_sem.at[i])
    for i in range(2 * ITERS - 1):
        left_buffer(edge_send.at[i], edge_send_sem.at[i])


def body(kernel, target_device, target_block, counts, traveltimes, prior_residual):
    n_lat, n_rad = lax.axis_size("lat"), lax.axis_size("rad")
    n = n_lat * n_rad
    rays_b, fanout, ray_len, cells = kernel.shape
    capacity = max(2, 2 * rays_b * fanout // n)
    slots = -(-capacity // 8) * 8
    halves = cells // LANES
    rows = halves * slots
    edges = 2 * halves * (MB_R + MB_L)
    payloads, sums, fields = 2 * ITERS, 2 * ITERS, 2 * ITERS - 1
    dma = pltpu.SemaphoreType.DMA
    vmem = pl.BlockSpec(memory_space=pltpu.VMEM)
    operands = (
        kernel, target_device.T, target_block.T, counts.reshape(1, rays_b),
        traveltimes, prior_residual,
    )
    return pl.pallas_call(
        functools.partial(lsqr_kernel, n_lat, n_rad, slots),
        out_shape=(
            jax.ShapeDtypeStruct((MB_R, MB_L, cells), F32),
            jax.ShapeDtypeStruct((rays_b, ray_len), F32),
        ),
        in_specs=[pl.BlockSpec(memory_space=pltpu.HBM)] * len(operands),
        out_specs=(vmem, vmem),
        scratch_shapes=[
            *[pltpu.VMEM(a.shape, a.dtype) for a in operands],
            pltpu.VMEM((payloads, n * rows, LANES), BF16),
            pltpu.VMEM((payloads, n * rows, LANES), BF16),
            pltpu.VMEM((sums, 1, LANES), F32),
            pltpu.VMEM((sums, n_rad, 1, LANES), F32),
            pltpu.VMEM((sums, 1, LANES), F32),
            pltpu.VMEM((sums, n_lat, 1, LANES), F32),
            pltpu.VMEM((fields, edges, LANES), F32),
            pltpu.VMEM((fields, edges, LANES), F32),
            pltpu.VMEM((n, 1, LANES), F32),
            pltpu.VMEM((n, 1, LANES), F32),
            dma((rays_b // GROUP,)),
            dma((len(operands) - 1,)),
            dma((payloads,)), dma((payloads,)),
            dma((sums,)), dma((sums,)), dma((sums,)), dma((sums,)),
            dma((fields,)), dma((fields,)),
            dma, dma,
        ],
        compiler_params=pltpu.CompilerParams(
            collective_id=0, has_side_effects=True, vmem_limit_bytes=48 * 1024 * 1024
        ),
        cost_estimate=pl.CostEstimate(
            flops=14 * kernel.size, bytes_accessed=2 * kernel.size, transcendentals=0
        ),
    )(*[pltpu.with_memory_space_constraint(a, pltpu.HBM) for a in operands])


def solution(mesh):
    in_specs = (
        P(("lat", "rad"), None, None, None),
        P(("lat", "rad"), None),
        P(("lat", "rad"), None),
        P(("lat", "rad")),
        P(("lat", "rad"), None),
        P(("lat", "rad"), None),
    )
    out_specs = (P("rad", "lat", None), P(("lat", "rad"), None))
    return jax.shard_map(body, mesh=mesh, in_specs=in_specs, out_specs=out_specs, check_vma=False)
```

```python
import functools

import jax
import jax.numpy as jnp
from jax import lax
from jax.experimental import pallas as pl
from jax.experimental.pallas import tpu as pltpu
from jax.sharding import PartitionSpec as P

ITERS = 3
MB_R = 8
MB_L = 16
FREEDOM = 4.0
DAMPING = 0.3
LANES = 128
GROUP = 8

F32 = jnp.float32
BF16 = jnp.bfloat16
MESH = pl.DeviceIdType.MESH


def iota(shape, dim):
    return lax.broadcasted_iota(jnp.int32, shape, dim)


def onehot(cond):
    return jnp.where(cond, 1.0, 0.0).astype(BF16)


def lsqr_kernel(
    n_lat, n_rad, slots,
    kernel_ref, target_hbm, block_hbm, counts_hbm, times_hbm, prior_hbm,
    update_ref, data_ref,
    tiles, target_ref, block_ref, counts_ref, times_ref, prior_ref,
    send, recv, rad_send, rad_recv, lat_send, lat_recv,
    edge_send, edge_recv, ids_send, ids_recv,
    tile_sem, small_sem, send_sem, recv_sem, rad_send_sem, rad_recv_sem,
    lat_send_sem, lat_recv_sem, edge_send_sem, edge_recv_sem, ids_send_sem, ids_recv_sem,
):
    n = n_lat * n_rad
    rays_b, fanout, ray_len, cells = tiles.shape
    entries = rays_b * fanout
    halves = cells // LANES
    rows = halves * slots
    num_blocks = MB_R * MB_L
    groups = rays_b // GROUP
    width = GROUP * ray_len
    lat, rad = lax.axis_index("lat"), lax.axis_index("rad")

    small = (
        (target_hbm, target_ref), (block_hbm, block_ref), (counts_hbm, counts_ref),
        (times_hbm, times_ref), (prior_hbm, prior_ref),
    )
    for i, (src, dst) in enumerate(small):
        pltpu.make_async_copy(src, dst, small_sem.at[i]).start()

    def tile_copy(g):
        part = pl.ds(g * GROUP, GROUP)
        return pltpu.make_async_copy(kernel_ref.at[part], tiles.at[part], tile_sem.at[g])

    for g in range(groups):
        tile_copy(g).start()

    rads = [lax.rem(rad + dr, n_rad) for dr in range(n_rad)]

    def each_lat(act):
        def go(i, carry):
            dl = n_lat // 2 + (2 * lax.rem(i, 2) - 1) * ((i + 1) // 2)
            act(dl, lax.rem(lat + dl, n_lat))
            return carry
        lax.fori_loop(0, n_lat - 1, go, 0)

    def each_partner(act):
        def row(dl, peer):
            here, there = dl * n_rad, (n_lat - dl) * n_rad
            for dr in range(n_rad):
                act(here + dr, there + (n_rad - dr) % n_rad, (peer, rads[dr]))
        each_lat(row)
        for dr in range(1, n_rad):
            act(dr, n_rad - dr, (lat, rads[dr]))

    barrier = pltpu.get_barrier_semaphore()
    each_partner(
        lambda here, there, device: pl.semaphore_signal(
            barrier, inc=1, device_id=device, device_id_type=MESH
        )
    )
    for i, (src, dst) in enumerate(small):
        pltpu.make_async_copy(src, dst, small_sem.at[i]).wait()

    square = (entries, entries)
    named = jnp.concatenate([target_ref[k:k + 1, :] for k in range(fanout)], axis=1)
    wanted = jnp.concatenate([block_ref[k:k + 1, :] for k in range(fanout)], axis=1)
    away_lat = named // n_rad - lat
    away_rad = named % n_rad - rad
    away_lat = jnp.where(away_lat < 0, away_lat + n_lat, away_lat)
    away_rad = jnp.where(away_rad < 0, away_rad + n_rad, away_rad)
    away_row = jnp.broadcast_to((away_lat * n_rad + away_rad).astype(F32), square)
    away_col = away_row.T
    wanted = jnp.broadcast_to(wanted.astype(F32), square).T[:, 0:1]
    earlier = (away_col == away_row) & (iota(square, 1) < iota(square, 0))
    rank = jnp.sum(jnp.where(earlier, 1.0, 0.0), axis=1, keepdims=True)
    place_col = away_col[:, 0:1] * rows + rank
    place_row = jnp.broadcast_to(place_col, square).T[0:1, :]
    place_cols = jnp.concatenate([place_col + h * slots for h in range(halves)], axis=0)
    place_rows = jnp.concatenate([place_row + h * slots for h in range(halves)], axis=1)
    spread = onehot(
        iota((n * rows, halves * entries), 0) == place_rows.astype(jnp.int32)
    )
    partner = onehot(iota((n, entries), 0) == away_row[0:1, :].astype(jnp.int32))
    marks = jnp.where(
        iota((entries, LANES), 1) == rank.astype(jnp.int32), wanted + 1.0, 0.0
    ).astype(BF16)
    ids = jnp.dot(partner, marks, preferred_element_type=F32)

    lane = iota((GROUP, width), 1)
    own = (lane // ray_len) == iota((GROUP, width), 0)
    ray = lane % ray_len
    eye = iota((rays_b, rays_b), 0) == iota((rays_b, rays_b), 1)
    count = jnp.sum(
        jnp.where(eye, jnp.broadcast_to(counts_ref[...], (rays_b, rays_b)).astype(F32), 0.0),
        axis=1, keepdims=True,
    ).astype(jnp.int32)

    def repeated(ref, g):
        part = ref[g * GROUP:(g + 1) * GROUP, :]
        return jnp.concatenate([part] * GROUP, axis=1)

    weights, data = [], []
    for g in range(groups):
        prior = repeated(prior_ref, g)
        valid = own & (ray < count[g * GROUP:(g + 1) * GROUP])
        w = jnp.where(valid, jnp.sqrt((FREEDOM + 1.0) / (FREEDOM + prior * prior)), 0.0)
        weights.append(w)
        data.append(w * repeated(times_ref, g))

    def total(parts):
        acc = parts[0] * parts[0]
        for p in parts[1:]:
            acc = acc + p * p
        return jnp.sum(jnp.sum(acc, axis=0, keepdims=True), axis=1, keepdims=True)

    pl.semaphore_wait(barrier, n - 1)

    def exchange(src, dst, size, s_sem, r_sem):
        def part(i):
            i = i * size
            return pl.ds(i if isinstance(i, int) else pl.multiple_of(i, size), size)

        def act(here, there, device):
            pltpu.make_async_remote_copy(
                src_ref=src.at[part(here)], dst_ref=dst.at[part(there)],
                send_sem=s_sem, recv_sem=r_sem, device_id=device, device_id_type=MESH,
            ).start()
        each_partner(act)

    def arrived(dst, size, sem, count=n):
        part = dst.at[pl.ds(size, (count - 1) * size)]
        pltpu.make_async_copy(part, part, sem).wait()

    def send_sum(i, value):
        row = jnp.broadcast_to(value, (1, LANES))
        rad_send[i] = row
        rad_recv[i, 0] = row
        for dr in range(1, n_rad):
            pltpu.make_async_remote_copy(
                src_ref=rad_send.at[i], dst_ref=rad_recv.at[i, n_rad - dr],
                send_sem=rad_send_sem.at[i], recv_sem=rad_recv_sem.at[i],
                device_id=(lat, rads[dr]), device_id_type=MESH,
            ).start()

    def pass_sum(i):
        arrived(rad_recv.at[i], 1, rad_recv_sem.at[i], n_rad)
        row = jnp.sum(rad_recv[i], axis=0)
        lat_send[i] = row
        lat_recv[i, 0] = row

        def act(dl, peer):
            pltpu.make_async_remote_copy(
                src_ref=lat_send.at[i], dst_ref=lat_recv.at[i, n_lat - dl],
                send_sem=lat_send_sem.at[i], recv_sem=lat_recv_sem.at[i],
                device_id=(peer, rad), device_id_type=MESH,
            ).start()
        each_lat(act)

    def get_sum(i):
        arrived(lat_recv.at[i], 1, lat_recv_sem.at[i], n_lat)
        return jnp.sum(lat_recv[i], axis=0)[:, 0:1]

    field4 = (halves, MB_R, MB_L, LANES)
    field = (halves * num_blocks, LANES)
    radial, lateral = halves * MB_L, halves * MB_R
    edge_parts = ((0, radial), (radial, radial), (2 * radial, lateral), (2 * radial + lateral, lateral))
    up = (lat, lax.rem(rad + n_rad - 1, n_rad))
    down = (lat, lax.rem(rad + 1, n_rad))
    left = (lax.rem(lat + n_lat - 1, n_lat), rad)
    right = (lax.rem(lat + 1, n_lat), rad)

    def send_edges(i, x):
        x4 = x.reshape(field4)
        edge_send[i, 0:radial] = x4[:, 0].reshape(radial, LANES)
        edge_send[i, radial:2 * radial] = x4[:, MB_R - 1].reshape(radial, LANES)
        edge_send[i, 2 * radial:2 * radial + lateral] = x4[:, :, 0].reshape(lateral, LANES)
        edge_send[i, 2 * radial + lateral:] = x4[:, :, MB_L - 1].reshape(lateral, LANES)
        for a, b, device in ((0, 1, up), (1, 0, down), (2, 3, left), (3, 2, right)):
            pltpu.make_async_remote_copy(
                src_ref=edge_send.at[i, pl.ds(*edge_parts[a])],
                dst_ref=edge_recv.at[i, pl.ds(*edge_parts[b])],
                send_sem=edge_send_sem.at[i], recv_sem=edge_recv_sem.at[i],
                device_id=device, device_id_type=MESH,
            ).start()

    def roughen(i, x):
        whole = edge_recv.at[i]
        pltpu.make_async_copy(whole, whole, edge_recv_sem.at[i]).wait()

        def edge(part, outside):
            start, size = edge_parts[part]
            return jnp.where(outside, 0.0, edge_recv[i, start:start + size])

        above = edge(0, rad == 0).reshape(halves, 1, MB_L, LANES)
        below = edge(1, rad == n_rad - 1).reshape(halves, 1, MB_L, LANES)
        before = edge(2, lat == 0)
        after = edge(3, lat == n_lat - 1)
        x4 = x.reshape(field4)
        radials = jnp.concatenate([above, x4[:, :-1]], axis=1) + jnp.concatenate(
            [x4[:, 1:], below], axis=1
        )

        def along(e):
            return jnp.broadcast_to(e[:, None, :], (lateral, MB_L, LANES)).reshape(field)

        block_l = iota(field, 0) % MB_L
        prev = jnp.where(block_l == 0, along(before), pltpu.roll(x, 1, 0))
        nxt = jnp.where(block_l == MB_L - 1, along(after), pltpu.roll(x, field[0] - 1, 0))
        return 4.0 * x - (radials.reshape(field) + prev + nxt)

    def tile_part(g, k):
        return tiles[g * GROUP:(g + 1) * GROUP, k].reshape(width, cells)

    def send_rows(i, values):
        send[i] = values.astype(BF16)
        recv[i, 0:rows] = send[i, 0:rows]
        exchange(send.at[i], recv.at[i], rows, send_sem.at[i], recv_sem.at[i])

    def adjoint(i, ray_values, sum_i=None):
        parts = [[None] * groups for _ in range(fanout)]
        for g in range(groups):
            if sum_i is None:
                tile_copy(g).wait()
            y = ray_values[g].astype(BF16)
            for k in range(fanout):
                parts[k][g] = jnp.dot(y, tile_part(g, k), preferred_element_type=F32)
        flat = [p for k in range(fanout) for p in parts[k]]
        stacked = jnp.concatenate(
            [p[:, h * LANES:(h + 1) * LANES] for h in range(halves) for p in flat], axis=0
        ).astype(BF16)
        if sum_i is not None:
            pass_sum(sum_i)
        send_rows(i, jnp.dot(spread, stacked, preferred_element_type=F32))

    def forward(i):
        arrived(recv.at[i], rows, recv_sem.at[i])
        blocks = jnp.dot(pick, recv[i], preferred_element_type=F32)
        out = []
        for g in range(groups):
            acc = None
            for k in range(fanout):
                at_row = k * rays_b + g * GROUP
                v = jnp.concatenate(
                    [
                        blocks[h * entries + at_row:h * entries + at_row + GROUP]
                        for h in range(halves)
                    ],
                    axis=1,
                ).astype(BF16)
                term = lax.dot_general(
                    v, tile_part(g, k), (((1,), (1,)), ((), ())), preferred_element_type=F32
                )
                acc = term if acc is None else acc + term
            out.append(acc)
        return out

    first_sum = total(data)
    id_rows = jnp.where(iota((n, LANES), 1) == slots, first_sum, ids)
    ids_send[...] = id_rows.reshape(n, 1, LANES)
    ids_recv[0] = ids_send[0]
    exchange(ids_send, ids_recv, 1, ids_send_sem, ids_recv_sem)

    adjoint(0, [w * d for w, d in zip(weights, data)])

    pick = onehot(
        iota((halves * entries, n * rows), 1) == place_cols.astype(jnp.int32)
    )

    arrived(ids_recv, 1, ids_recv_sem)
    got = ids_recv[...].reshape(n, LANES)
    beta = jnp.sqrt(jnp.sum(got, axis=0, keepdims=True)[:, slots:slots + 1])
    slot_rows = (n * rows, LANES)
    each = jnp.broadcast_to(got[:, None, :], (n, rows, LANES)).reshape(slot_rows)
    each = jnp.where(iota(slot_rows, 1) == iota(slot_rows, 0) % slots, each, 0.0)
    block_id = jnp.sum(each, axis=1, keepdims=True).astype(jnp.int32)
    asked = jnp.where(iota(slot_rows, 1) + 1 == block_id, 1.0, 0.0)
    half = (iota(slot_rows, 0) % rows) // slots
    served = jnp.concatenate([jnp.where(half == h, asked, 0.0) for h in range(halves)], axis=1)
    gather = served.astype(BF16)
    collect = served.T.astype(BF16)

    def collected(i):
        arrived(recv.at[i], rows, recv_sem.at[i])
        return jnp.dot(collect, recv[i], preferred_element_type=F32)

    x = collected(0) / beta
    data = [d / beta for d in data]
    phi_bar = beta
    round_i, sum_i, edge_i = 1, 0, 0
    pen = search = update = None
    for sweep in range(ITERS):
        send_rows(round_i, jnp.dot(gather, x.astype(BF16), preferred_element_type=F32))
        send_sum(sum_i, total([x]))
        send_edges(edge_i, x)
        pass_sum(sum_i)
        rough = DAMPING * roughen(edge_i, x)
        products = forward(round_i)
        alpha = jnp.sqrt(get_sum(sum_i))
        inverse = 1.0 / alpha
        data = [w * (p * inverse) - alpha * d for w, p, d in zip(weights, products, data)]
        v = x * inverse
        pen_new = inverse * rough
        pen = pen_new if pen is None else pen_new - alpha * pen
        round_i, sum_i, edge_i = round_i + 1, sum_i + 1, edge_i + 1
        if sweep == 0:
            search = v
            rho_bar = alpha
        else:
            search = v - (sine * alpha / rho) * search
            rho_bar = -cosine * alpha
        last = sweep == ITERS - 1
        acc = total(data) + total([pen])
        send_sum(sum_i, acc)
        if not last:
            send_edges(edge_i, pen)
            adjoint(round_i, [w * d for w, d in zip(weights, data)], sum_i)
        else:
            pass_sum(sum_i)
        beta = jnp.sqrt(get_sum(sum_i))
        inverse = 1.0 / beta
        data = [d * inverse for d in data]
        rho = jnp.sqrt(rho_bar * rho_bar + beta * beta)
        cosine, sine = rho_bar / rho, beta / rho
        phi = cosine * phi_bar
        phi_bar = sine * phi_bar
        step = (phi / rho) * search
        update = step if update is None else update + step
        if not last:
            rest = (DAMPING * inverse) * roughen(edge_i, pen) - beta * v
            pen = pen * inverse
            x = collected(round_i) * inverse + rest
            round_i, edge_i = round_i + 1, edge_i + 1
        sum_i += 1

    for h in range(halves):
        part = update[h * num_blocks:(h + 1) * num_blocks]
        update_ref[:, :, h * LANES:(h + 1) * LANES] = part.reshape(MB_R, MB_L, LANES)
    for g in range(groups):
        acc = data[g][:, 0:ray_len]
        for i in range(1, GROUP):
            acc = acc + data[g][:, i * ray_len:(i + 1) * ray_len]
        data_ref[g * GROUP:(g + 1) * GROUP, :] = acc

    def left_buffer(ref, sem):
        pltpu.make_async_copy(ref, ref, sem).wait()

    left_buffer(ids_send.at[pl.ds(1, n - 1)], ids_send_sem)
    for i in range(2 * ITERS):
        left_buffer(send.at[i, pl.ds(rows, (n - 1) * rows)], send_sem.at[i])
    for i in range(2 * ITERS):
        left_buffer(rad_recv.at[i, pl.ds(1, n_rad - 1)], rad_send_sem.at[i])
        left_buffer(lat_recv.at[i, pl.ds(1, n_lat - 1)], lat_send_sem.at[i])
    for i in range(2 * ITERS - 1):
        left_buffer(edge_send.at[i], edge_send_sem.at[i])


def body(kernel, target_device, target_block, counts, traveltimes, prior_residual):
    n_lat, n_rad = lax.axis_size("lat"), lax.axis_size("rad")
    n = n_lat * n_rad
    rays_b, fanout, ray_len, cells = kernel.shape
    capacity = max(2, 2 * rays_b * fanout // n)
    slots = -(-capacity // 8) * 8
    halves = cells // LANES
    rows = halves * slots
    edges = 2 * halves * (MB_R + MB_L)
    payloads, sums, fields = 2 * ITERS, 2 * ITERS, 2 * ITERS - 1
    dma = pltpu.SemaphoreType.DMA
    vmem = pl.BlockSpec(memory_space=pltpu.VMEM)
    operands = (
        kernel, target_device.T, target_block.T, counts.reshape(1, rays_b),
        traveltimes, prior_residual,
    )
    return pl.pallas_call(
        functools.partial(lsqr_kernel, n_lat, n_rad, slots),
        out_shape=(
            jax.ShapeDtypeStruct((MB_R, MB_L, cells), F32),
            jax.ShapeDtypeStruct((rays_b, ray_len), F32),
        ),
        in_specs=[pl.BlockSpec(memory_space=pltpu.HBM)] * len(operands),
        out_specs=(vmem, vmem),
        scratch_shapes=[
            *[pltpu.VMEM(a.shape, a.dtype) for a in operands],
            pltpu.VMEM((payloads, n * rows, LANES), BF16),
            pltpu.VMEM((payloads, n * rows, LANES), BF16),
            pltpu.VMEM((sums, 1, LANES), F32),
            pltpu.VMEM((sums, n_rad, 1, LANES), F32),
            pltpu.VMEM((sums, 1, LANES), F32),
            pltpu.VMEM((sums, n_lat, 1, LANES), F32),
            pltpu.VMEM((fields, edges, LANES), F32),
            pltpu.VMEM((fields, edges, LANES), F32),
            pltpu.VMEM((n, 1, LANES), F32),
            pltpu.VMEM((n, 1, LANES), F32),
            dma((rays_b // GROUP,)),
            dma((len(operands) - 1,)),
            dma((payloads,)), dma((payloads,)),
            dma((sums,)), dma((sums,)), dma((sums,)), dma((sums,)),
            dma((fields,)), dma((fields,)),
            dma, dma,
        ],
        compiler_params=pltpu.CompilerParams(
            collective_id=0, has_side_effects=True, vmem_limit_bytes=48 * 1024 * 1024
        ),
        cost_estimate=pl.CostEstimate(
            flops=14 * kernel.size, bytes_accessed=2 * kernel.size, transcendentals=0
        ),
    )(*[pltpu.with_memory_space_constraint(a, pltpu.HBM) for a in operands])


def solution(mesh):
    in_specs = (
        P(("lat", "rad"), None, None, None),
        P(("lat", "rad"), None),
        P(("lat", "rad"), None),
        P(("lat", "rad")),
        P(("lat", "rad"), None),
        P(("lat", "rad"), None),
    )
    out_specs = (P("rad", "lat", None), P(("lat", "rad"), None))
    return jax.shard_map(body, mesh=mesh, in_specs=in_specs, out_specs=out_specs, check_vma=False)
```
